128 devices in a mesh: row: 8 (over y, core), col: 16 (over z, x).
Axes of the slice: x: 4, y: 4, z: 4, core: 2. Of those that a mesh axis runs over, the one named last changes fastest.
Arguments:
- object_field: float32 [2048, 2, 4096], P('row', None, 'col'), may hold values from -6 to 6
- probe_modes: float32 [4, 256, 2, 256], replicated, may hold values from -1.5 to 1.5
- amplitudes: bfloat16 [8, 128, 256, 256], P('row', 'col'), may hold values from 0 to 2
- positions: int32 [8, 128, 2], P('row', 'col'), may hold values from 0 to 4095, as said below
- counts: int32 [8, 16], P('row', 'col'), may hold values from 0 to 8, as said below
Outputs:
- update: float32 [2048, 2, 4096], P('row', None, 'col')
The draws below stay inside these ranges and needn't reach their ends.
Inputs may be any that keep to these rules, and one draw needn't show every extreme that they name: counts[r, c] is the number of positions held by the owner at mesh row r, column c, in its first counts[r, c] slots. The 64 positions of row band r (object rows r * 256 to (r + 1) * 256 - 1) are held in scan order by the owners of mesh row r, owner 0 first, so the counts of a row sum to 64; in every row some owner holds exactly 8. A live slot's center lies in its owner's row band; exactly 4 centers of the band lie in each tile of it (tile columns c * 256 to (c + 1) * 256 - 1), and every center held by the owner in mesh column c lies in tile column c or c + 1. Entries of slots at or beyond an owner's count are not positions and are ignored.
All inputs are finite; a program needn't handle non-finite values.
Results may differ from the reference program's by a relative error of at most 0.0085.
Values may be sent and summed in bfloat16 or wider, within the bound.
A program may use at most 128 MiB of HBM per device.

```python
import jax
import jax.numpy as jnp
from jax import lax

M = 256
MODES = 4
TR = 256
TC = 256
PER_TILE = 4
SLOTS = 8
NR = 2048
NC = 4096
N_ROW = 8
N_COL = 16


def scan_layout(key):
    band_total = N_COL * PER_TILE
    excess = jax.random.randint(jax.random.fold_in(key, 11), (N_ROW, N_COL), 0, PER_TILE + 1)
    columns = jnp.arange(N_COL, dtype=jnp.int32)
    busiest = jax.random.randint(jax.random.fold_in(key, 12), (N_ROW, 1), 0, N_COL - 1)
    excess = jnp.where(columns[None, :] == busiest, PER_TILE, excess)
    excess = jnp.where(columns[None, :] == busiest - 1, 0, excess)
    excess = jnp.where(columns[None, :] == N_COL - 1, 0, excess)
    before = jnp.concatenate([jnp.zeros((N_ROW, 1), jnp.int32), excess[:, :-1]], axis=1)
    holding = PER_TILE + excess - before
    starts = columns[None, :] * PER_TILE + before
    stride = TR // PER_TILE
    scan_order = jnp.arange(band_total, dtype=jnp.int32)
    band_rows = jnp.arange(N_ROW, dtype=jnp.int32)
    center_row = band_rows[:, None] * TR + (scan_order % PER_TILE)[None, :] * stride + jax.random.randint(jax.random.fold_in(key, 13), (N_ROW, band_total), 0, stride)
    center_col = (scan_order // PER_TILE)[None, :] * TC + jax.random.randint(jax.random.fold_in(key, 14), (N_ROW, band_total), 0, TC)
    slot_ids = jnp.arange(SLOTS, dtype=jnp.int32)
    scan_index = starts[:, :, None] + slot_ids[None, None, :]
    is_alive = slot_ids[None, None, :] < holding[:, :, None]
    safe_index = jnp.minimum(scan_index, band_total - 1).reshape(N_ROW, N_COL * SLOTS)
    held_row = jnp.take_along_axis(center_row, safe_index, axis=1).reshape(N_ROW, N_COL, SLOTS)
    held_col = jnp.take_along_axis(center_col, safe_index, axis=1).reshape(N_ROW, N_COL, SLOTS)
    spare_row = band_rows[:, None, None] * TR + jax.random.randint(jax.random.fold_in(key, 15), (N_ROW, N_COL, SLOTS), 0, TR)
    spare_col = columns[None, :, None] * TC + jax.random.randint(jax.random.fold_in(key, 16), (N_ROW, N_COL, SLOTS), 0, TC)
    final_row = jnp.where(is_alive, held_row, spare_row)
    final_col = jnp.where(is_alive, held_col, spare_col)
    places = jnp.stack([final_row, final_col], axis=-1).reshape(N_ROW, N_COL * SLOTS, 2)
    return (holding.astype(jnp.int32), places.astype(jnp.int32))


def draw_positions(key, part):
    holding, places = scan_layout(key)
    return places


def draw_counts(key, part):
    holding, places = scan_layout(key)
    return holding


def block_levels(stream_key, shape, pieces, smallest, high):
    def one(position, shards_of):
        steps = jax.random.uniform(jax.random.fold_in(jax.random.fold_in(stream_key, 6), position), (shards_of,), jnp.float32, smallest / len(pieces), high / len(pieces))
        return jnp.repeat(jnp.exp(steps), shape[position] // shards_of).reshape((-1,) + (1,) * (len(shape) - position - 1))

    factor_of = one(*pieces[0])
    for cut in pieces[1:]:
        factor_of = factor_of * one(*cut)
    return factor_of


def centred(stream_key, dims, deviation, bound, pieces=(), kind=jnp.bfloat16):
    array = deviation * jax.random.normal(stream_key, dims, jnp.float32)
    if pieces:
        array = array * block_levels(stream_key, dims, pieces, -0.22, 0.18)
    return jnp.clip(array, -bound, bound).astype(kind)


def setup_inputs(seed: int = 0) -> dict:
    key_list = jax.random.split(jax.random.key(seed), 6)
    return {
        "object_field": centred(key_list[0], (NR, 2, NC), 1.0, 6.0, ((0, 8), (2, 16)), jnp.float32),
        "probe_modes": centred(key_list[1], (MODES, M, 2, M), 0.25, 1.5, (), jnp.float32),
        "amplitudes": jnp.clip(2.0 * jax.random.uniform(key_list[2], (N_ROW, N_COL * SLOTS, M, M), jnp.float32) ** block_levels(key_list[2], (N_ROW, N_COL * SLOTS, M, M), ((0, 8), (1, 16)), -0.2, 0.2), 0.0, 2.0).astype(jnp.bfloat16),
        "positions": draw_positions(jax.random.fold_in(key_list[5], 71), 0),
        "counts": draw_counts(jax.random.fold_in(key_list[5], 71), 0),
    }


floor_amplitude = 0.25
ridge_weight = 1.0

def dft_tables(extent):
    indices = jnp.arange(extent, dtype=jnp.int32)
    phase_steps = indices[:, None] * indices[None, :] % extent
    angles = phase_steps.astype(jnp.float32) * (2.0 * jnp.pi / extent)
    scaling = 1.0 / jnp.sqrt(jnp.float32(extent))
    cosine = (jnp.cos(angles) * scaling).astype(jnp.bfloat16)
    sine_table = (jnp.sin(angles) * scaling).astype(jnp.bfloat16)
    return (cosine, sine_table)

def transform_window(window, amplitude, probe_pair, cosine, sine_table):
    extent = window.shape[0]
    probe_re = probe_pair[:, :, :extent]
    probe_im = probe_pair[:, :, extent:]
    object_re = window[None, :, :extent]
    object_im = window[None, :, extent:]
    exit_wave = jnp.concatenate([probe_re * object_re - probe_im * object_im, probe_re * object_im + probe_im * object_re], axis=-1).astype(jnp.bfloat16)
    forward_table = jnp.concatenate([jnp.concatenate([cosine, -sine_table], axis=1), jnp.concatenate([sine_table, cosine], axis=1)], axis=0)
    inverse_table = jnp.concatenate([jnp.concatenate([cosine, sine_table], axis=1), jnp.concatenate([-sine_table, cosine], axis=1)], axis=0)
    cosine_full = cosine.astype(jnp.float32)
    sine_full = sine_table.astype(jnp.float32)
    half_done = jnp.einsum('kpq,qv->kpv', exit_wave.astype(jnp.float32), forward_table.astype(jnp.float32)).astype(jnp.bfloat16)
    first_part = jnp.einsum('up,kpq->kuq', cosine_full, half_done.astype(jnp.float32))
    second_part = jnp.einsum('up,kpq->kuq', sine_full, half_done.astype(jnp.float32))
    far_re = first_part[..., :extent] + second_part[..., extent:]
    far_im = first_part[..., extent:] - second_part[..., :extent]
    intensity = lax.optimization_barrier(jnp.sum(far_re * far_re + far_im * far_im, axis=0))
    factor = 1.0 - amplitude.astype(jnp.float32) / jnp.maximum(jnp.sqrt(intensity), floor_amplitude)
    residue = jnp.concatenate([far_re * factor, far_im * factor], axis=-1).astype(jnp.bfloat16)
    first_back = jnp.einsum('up,kpq->kuq', cosine_full, residue.astype(jnp.float32))
    second_back = jnp.einsum('up,kpq->kuq', sine_full, residue.astype(jnp.float32))
    near_field = jnp.concatenate([first_back[..., :extent] - second_back[..., extent:], first_back[..., extent:] + second_back[..., :extent]], axis=-1).astype(jnp.bfloat16)
    returned = jnp.einsum('kpq,qv->kpv', near_field.astype(jnp.float32), inverse_table.astype(jnp.float32))
    back_re = returned[..., :extent]
    back_im = returned[..., extent:]
    grad_re = lax.optimization_barrier(jnp.sum(probe_re * back_re + probe_im * back_im, axis=0))
    grad_im = lax.optimization_barrier(jnp.sum(probe_re * back_im - probe_im * back_re, axis=0))
    return jnp.stack([grad_re, grad_im], axis=1)

def reference(object_field, probe_modes, amplitudes, positions, counts):
    extent = probe_modes.shape[1]
    half_width = extent // 2
    rows_all = object_field.shape[0]
    cols_all = object_field.shape[2]
    cosine, sine_table = dft_tables(extent)
    probe_pair = probe_modes.reshape(probe_modes.shape[0], extent, 2 * extent)
    lighting = lax.optimization_barrier(jnp.sum(probe_modes[:, :, 0, :] ** 2 + probe_modes[:, :, 1, :] ** 2, axis=0))
    padded = jnp.pad(object_field, ((half_width, half_width), (0, 0), (half_width, half_width)))
    slot_index = jnp.arange(N_COL * SLOTS, dtype=jnp.int32)
    live_mask = (slot_index % SLOTS)[None, :] < jnp.repeat(counts, SLOTS, axis=1)
    flat_positions = positions.reshape(-1, 2)
    flat_live = live_mask.reshape(-1).astype(jnp.float32)
    flat_amplitudes = amplitudes.reshape(-1, extent, extent)

    def visit_slot(canvas, operands):
        location, alive_weight, amplitude = operands
        corner = (location[0], jnp.int32(0), location[1])
        window = lax.dynamic_slice(padded, corner, (extent, 2, extent)).reshape(extent, 2 * extent)
        gradient = transform_window(window, amplitude, probe_pair, cosine, sine_table)
        contribution = jnp.concatenate([gradient, lighting[:, None, :]], axis=1) * alive_weight
        current = lax.dynamic_slice(canvas, corner, (extent, 3, extent))
        return (lax.dynamic_update_slice(canvas, current + contribution, corner), None)
    canvas = jnp.zeros((rows_all + extent, 3, cols_all + extent), jnp.float32)
    canvas, _ = lax.scan(visit_slot, canvas, (flat_positions, flat_live, flat_amplitudes))
    interior = canvas[half_width:half_width + rows_all, :, half_width:half_width + cols_all]
    return interior[:, :2, :] / (interior[:, 2:, :] + ridge_weight)
```

```python
import functools

import jax
import jax.numpy as jnp
import numpy as np
from jax import lax
from jax.experimental import pallas as pl
from jax.experimental.pallas import tpu as pltpu
from jax.sharding import PartitionSpec as P

MESH = pl.DeviceIdType.MESH
F32 = jnp.float32
BF16 = jnp.bfloat16

floor_amplitude = 0.25
ridge_weight = 1.0

POS, CNT = 0, 1
OBJ_X = 2
OBJ_Y = 4
CORNER = 6
AMP = 10
W_Y = 14
W_X = 16
G_Y = 18
G_X = 22
COPIES = 26


def tables(extent):
    half = extent // 2
    steps = np.arange(extent)
    turns = np.outer(np.arange(half), steps) % extent
    scale = 1.0 / np.sqrt(extent)
    cosine = np.cos(2.0 * np.pi * turns / extent) * scale
    sine = np.sin(2.0 * np.pi * turns / extent) * scale
    forward = []
    for parity in range(2):
        c, s = cosine[:, parity::2], sine[:, parity::2]
        forward.append(np.block([[c, -s], [s, c]]))
    order = np.concatenate([steps[0::2], steps[1::2]])
    permute = np.eye(extent)[order]
    stack = [forward[0], forward[1], forward[0].T, forward[1].T, permute, permute.T]
    return np.stack(stack).astype(np.float32).astype(jnp.bfloat16)


def dot(a, b):
    return jnp.dot(a, b, preferred_element_type=F32)


def kernel(
    n_row, n_col, slots, modes,
    obj_hbm, probe_hbm, amp_hbm, tab_hbm, pos, cnt, out,
    obj, probe, amps, tab, pp, light, ext, win,
    sx, rx, sy, ry, rc, sa, ra, left_pos, left_cnt, table,
    far, fac, grad, pg, pw, cv, cw,
    wsy, wry, wsx, wrx, gsy, gry, gsx, grx,
    lsem, ssem, rsem,
):
    row, col = lax.axis_index("row"), lax.axis_index("col")
    right, left = lax.rem(col + 1, n_col), lax.rem(col + n_col - 1, n_col)
    down, up = lax.rem(row + 1, n_row), lax.rem(row + n_row - 1, n_row)
    to_right, to_left, to_down, to_up = (row, right), (row, left), (down, col), (up, col)

    def remote(number, src, dst, target):
        return pltpu.make_async_remote_copy(
            src_ref=src, dst_ref=dst, send_sem=ssem.at[number], recv_sem=rsem.at[number],
            device_id=target, device_id_type=MESH,
        )

    local = [
        pltpu.make_async_copy(obj_hbm, obj, lsem.at[0]),
        pltpu.make_async_copy(amp_hbm, amps.at[pl.ds(0, slots)], lsem.at[1]),
        pltpu.make_async_copy(probe_hbm, probe, lsem.at[2]),
        pltpu.make_async_copy(tab_hbm, tab, lsem.at[3]),
    ]
    for copy in local:
        copy.start()

    barrier = pltpu.get_barrier_semaphore()
    for target in (to_right, to_left, to_down, to_up):
        pl.semaphore_signal(barrier, inc=1, device_id=target, device_id_type=MESH)

    local[0].wait()
    for c in range(2):
        for b in range(2):
            ext[c, 1 + b, 128:384, :] = obj[pl.ds(2 * b + c, 256, stride=4), :]
    for c in range(2):
        sx[0, c] = ext[c, 2, 128:384, :].astype(BF16)
        sx[1, c] = ext[c, 1, 128:384, :].astype(BF16)
    for c in range(2):
        for b in range(2):
            sy[0, c, b] = ext[c, 1 + b, 256:384, :].astype(BF16)
            sy[1, c, b] = ext[c, 1 + b, 128:256, :].astype(BF16)

    pl.semaphore_wait(barrier, 4)
    sent = []

    def send(*arguments):
        copy = remote(*arguments)
        copy.start()
        sent.append(copy)
        return copy

    pos_copy = send(POS, pos, left_pos, to_right)
    cnt_copy = send(CNT, cnt, left_cnt, to_right)
    obj_x = [send(OBJ_X, sx.at[0], rx.at[0], to_right), send(OBJ_X + 1, sx.at[1], rx.at[1], to_left)]
    obj_y = [send(OBJ_Y, sy.at[0], ry.at[0], to_down), send(OBJ_Y + 1, sy.at[1], ry.at[1], to_up)]

    def ranked(ref, count, tile):
        rank = jnp.int32(0)
        picked = [[jnp.int32(0)] * 3 for _ in range(4)]
        for i in range(slots):
            y, x = ref[0, i, 0], ref[0, i, 1]
            here = jnp.where((i < count) & ((x >> 8) == tile), 1, 0)
            for j in range(4):
                hit = jnp.where(rank == j, here, 0)
                picked[j] = [old + hit * new for old, new in zip(picked[j], (i, y, x))]
            rank = rank + here
        return picked, rank

    going, _ = ranked(pos, cnt[0, 0], col + 1)
    local[1].wait()
    for j in range(4):
        sa[j] = amps[going[j][0] & (slots - 1)]
    for j in range(4):
        send(AMP + j, sa.at[j], ra.at[j], to_right)

    local[2].wait()
    for k in range(modes):
        for c in range(2):
            for b in range(2):
                pp[k, c, b] = probe[pl.ds(k * 1024 + 2 * b + c, 256, stride=4), :]
    for b in range(2):
        total = None
        for k in range(modes):
            for c in range(2):
                term = pp[k, c, b] * pp[k, c, b]
                total = term if total is None else total + term
        light[b] = total

    pg[...] = jnp.zeros_like(pg)
    pw[...] = jnp.zeros_like(pw)
    cv[...] = jnp.zeros_like(cv)
    cw[...] = jnp.zeros_like(cw)
    for j in range(4):
        amps[slots + j] = jnp.zeros((256, 256), BF16)

    pos_copy.wait_recv()
    cnt_copy.wait_recv()
    home, n_home = ranked(pos, cnt[0, 0], col)
    came, _ = ranked(left_pos, left_cnt[0, 0], col)
    for j in range(4):
        for i in range(2):
            table[3 + i, j] = came[j][1 + i]
    for j in range(4):
        from_left = j >= n_home
        there = jnp.clip(j - n_home, 0, 3)
        table[0, j] = jnp.where(from_left, slots + there, home[j][0])
        for i in range(2):
            table[1 + i, j] = jnp.where(from_left, table[3 + i, there], home[j][1 + i]) & 255

    corners = []
    for side in range(2):
        obj_x[side].wait_recv()
        corners.append(send(CORNER + side, rx.at[side, :, pl.ds(128, 128)], rc.at[0, side], to_down))
        corners.append(send(CORNER + 2 + side, rx.at[side, :, pl.ds(0, 128)], rc.at[1, side], to_up))

    lanes = lax.broadcasted_iota(jnp.int32, (256, 128), 1)

    def spread(ref, pieces, shift):
        keep = lanes >= shift
        low, high = (pltpu.roll(piece, shift, 1) for piece in pieces)
        ref[1, 256:512, :] = jnp.where(keep, low, 0.0)
        ref[2, 256:512, :] = jnp.where(keep, high, low)
        ref[3, 256:512, :] = jnp.where(keep, 0.0, high)

    def place(canvas, ref, y, block):
        for b in range(4):
            canvas[b] += ref[b - block + 1, pl.ds(256 - y, 512), :]

    def weigh(j, carry):
        y, x = table[1, j], table[2, j]
        spread(pw, [light[0], light[1]], x & 127)
        place(cw, pw, y, x >> 7)
        return carry

    lax.fori_loop(0, 4, weigh, 0)
    for b in range(4):
        wsy[0, b] = cw[b, 384:512, :].astype(BF16)
        wsy[1, b] = cw[b, 0:128, :].astype(BF16)
    w_y = [send(W_Y, wsy.at[0], wry.at[0], to_down), send(W_Y + 1, wsy.at[1], wry.at[1], to_up)]

    from_left_on = jnp.where(col > 0, 1.0, 0.0).astype(F32)
    from_right_on = jnp.where(col < n_col - 1, 1.0, 0.0).astype(F32)
    from_up_on = jnp.where(row > 0, 1.0, 0.0).astype(F32)
    from_down_on = jnp.where(row < n_row - 1, 1.0, 0.0).astype(F32)
    x_on, y_on = (from_left_on, from_right_on), (from_up_on, from_down_on)
    for side in range(2):
        for c in range(2):
            ext[c, 3 * side, 128:384, :] = rx[side, c].astype(F32) * x_on[side]
    for end in range(2):
        obj_y[end].wait_recv()
        first = 384 * end
        for c in range(2):
            for b in range(2):
                ext[c, 1 + b, first : first + 128, :] = ry[end, c, b].astype(F32) * y_on[end]
    for copy in corners:
        copy.wait_recv()
    for end in range(2):
        first = 384 * end
        for side in range(2):
            for c in range(2):
                ext[c, 3 * side, first : first + 128, :] = rc[end, side, c].astype(F32) * (y_on[end] * x_on[side])

    local[3].wait()

    def slot(j, carry):
        y, x = table[1, j], table[2, j]
        block, shift = x >> 7, x & 127
        keep = lanes >= shift
        for c in range(2):
            for b in range(2):
                near = ext[c, block + b, pl.ds(y, 256), :]
                far_off = ext[c, block + b + 1, pl.ds(y, 256), :]
                win[c, b] = pltpu.roll(jnp.where(keep, near, far_off), (128 - shift) & 127, 1)
        for k in range(modes):
            waves = []
            for b in range(2):
                p_re, p_im, w_re, w_im = pp[k, 0, b], pp[k, 1, b], win[0, b], win[1, b]
                waves.append((p_re * w_re - p_im * w_im, p_re * w_im + p_im * w_re))
            (lo_re, lo_im), (hi_re, hi_im) = waves
            even = jnp.concatenate([lo_re + hi_re, lo_im + hi_im], axis=1).astype(BF16)
            odd = jnp.concatenate([lo_re - hi_re, lo_im - hi_im], axis=1).astype(BF16)
            h_even, h_odd = dot(even, tab[0]), dot(odd, tab[1])
            for parity in range(2):
                if parity == 0:
                    e, o = h_even[:128] + h_even[128:], h_odd[:128] + h_odd[128:]
                else:
                    e, o = h_even[:128] - h_even[128:], h_odd[:128] - h_odd[128:]
                stacked = jnp.concatenate(
                    [
                        jnp.concatenate([e[:, :128], o[:, :128]], axis=1),
                        jnp.concatenate([e[:, 128:], o[:, 128:]], axis=1),
                    ],
                    axis=0,
                ).astype(BF16)
                far[parity, k] = dot(tab[2 + parity], stacked)

        pltpu.make_async_remote_copy(
            src_ref=sa.at[j], dst_ref=ra.at[j], send_sem=ssem.at[AMP + j], recv_sem=rsem.at[AMP + j],
            device_id=to_right, device_id_type=MESH,
        ).wait_recv()
        amps[slots + j] = ra[j]
        rows_split = dot(tab[4], amps[table[0, j]]).astype(BF16)
        amplitude = dot(rows_split, tab[5])
        for parity in range(2):
            intensity = None
            for k in range(modes):
                re, im = far[parity, k, :128, :], far[parity, k, 128:, :]
                term = re * re + im * im
                intensity = term if intensity is None else intensity + term
            held = lax.rsqrt(jnp.maximum(intensity, floor_amplitude * floor_amplitude))
            fac[parity] = 1.0 - amplitude[128 * parity : 128 * parity + 128] * held

        for k in range(modes):
            parts = []
            for parity in range(2):
                factor = jnp.concatenate([fac[parity], fac[parity]], axis=0)
                parts.append(dot(tab[parity], (far[parity, k] * factor).astype(BF16)))
            low, high = parts[0] + parts[1], parts[0] - parts[1]
            ends = []
            for parity in range(2):
                cut = slice(128 * parity, 128 * parity + 128)
                near = jnp.concatenate(
                    [
                        jnp.concatenate([low[:128, cut], low[128:, cut]], axis=1),
                        jnp.concatenate([high[:128, cut], high[128:, cut]], axis=1),
                    ],
                    axis=0,
                ).astype(BF16)
                ends.append(dot(near, tab[2 + parity]))
            for b in range(2):
                back = ends[0] + ends[1] if b == 0 else ends[0] - ends[1]
                b_re, b_im = back[:, :128], back[:, 128:]
                p_re, p_im = pp[k, 0, b], pp[k, 1, b]
                g_re, g_im = p_re * b_re + p_im * b_im, p_re * b_im - p_im * b_re
                if k == 0:
                    grad[0, b], grad[1, b] = g_re, g_im
                else:
                    grad[0, b] += g_re
                    grad[1, b] += g_im
        for c in range(2):
            spread(pg.at[c], [grad[c, 0], grad[c, 1]], shift)
            place(cv.at[c], pg.at[c], y, block)
        return carry

    lax.fori_loop(0, 4, slot, 0)

    g_y = []
    for c in range(2):
        for b in range(4):
            gsy[c, 0, b] = cv[c, b, 384:512, :].astype(BF16)
            gsy[c, 1, b] = cv[c, b, 0:128, :].astype(BF16)
        g_y.append(send(G_Y + 2 * c, gsy.at[c, 0], gry.at[c, 0], to_down))
        g_y.append(send(G_Y + 2 * c + 1, gsy.at[c, 1], gry.at[c, 1], to_up))

    for copy in w_y:
        copy.wait_recv()
    for end in range(2):
        cut = slice(128 + 128 * end, 256 + 128 * end)
        for b in range(4):
            cw[b, cut, :] += wry[end, b].astype(F32) * y_on[end]
    wsx[0] = cw[3, 128:384, :].astype(BF16)
    wsx[1] = cw[0, 128:384, :].astype(BF16)
    w_x = [send(W_X, wsx.at[0], wrx.at[0], to_right), send(W_X + 1, wsx.at[1], wrx.at[1], to_left)]

    g_x = []
    for c in range(2):
        for end in range(2):
            g_y[2 * c + end].wait_recv()
            cut = slice(128 + 128 * end, 256 + 128 * end)
            for b in (0, 3):
                side = 0 if b == 3 else 1
                piece = cv[c, b, cut, :] + gry[c, end, b].astype(F32) * y_on[end]
                gsx[c, side, 128 * end : 128 * end + 128, :] = piece.astype(BF16)
        g_x.append(send(G_X + 2 * c, gsx.at[c, 0], grx.at[c, 0], to_right))
        g_x.append(send(G_X + 2 * c + 1, gsx.at[c, 1], grx.at[c, 1], to_left))
        for end in range(2):
            cut = slice(128 + 128 * end, 256 + 128 * end)
            for b in (1, 2):
                cv[c, b, cut, :] += gry[c, end, b].astype(F32) * y_on[end]
    for b in range(2):
        w_x[b].wait_recv()
        weight = cw[1 + b, 128:384, :] + wrx[b].astype(F32) * x_on[b]
        cw[1 + b, 128:384, :] = 1.0 / (weight + ridge_weight)
    for c in range(2):
        for b in range(2):
            g_x[2 * c + b].wait_recv()
            total = cv[c, 1 + b, 128:384, :] + grx[c, b].astype(F32) * x_on[b]
            out[pl.ds(2 * b + c, 256, stride=4), :] = total * cw[1 + b, 128:384, :]

    for copy in sent:
        copy.wait_send()


def on_device(n_row, n_col, object_field, probe_modes, amplitudes, positions, counts):
    modes, extent = probe_modes.shape[0], probe_modes.shape[1]
    slots = amplitudes.shape[1]
    half = extent // 2
    obj = object_field.reshape(extent, 2, 2, half).transpose(0, 2, 1, 3).reshape(4 * extent, half)
    probe = probe_modes.reshape(modes, extent, 2, 2, half).transpose(0, 1, 3, 2, 4)
    probe = probe.reshape(modes * 4 * extent, half)
    tab = jnp.asarray(tables(extent))
    big = 2 * extent
    vmem, anywhere = pltpu.VMEM, pl.BlockSpec(memory_space=pl.ANY)
    scratch = [
        vmem((4 * extent, half), F32),
        vmem((modes * 4 * extent, half), F32),
        vmem((slots + 4, extent, extent), BF16),
        vmem((6, extent, extent), BF16),
        vmem((modes, 2, 2, extent, half), F32),
        vmem((2, extent, half), F32),
        vmem((2, 4, big, half), F32),
        vmem((2, 2, extent, half), F32),
        vmem((2, 2, extent, half), BF16),
        vmem((2, 2, extent, half), BF16),
        vmem((2, 2, 2, half, half), BF16),
        vmem((2, 2, 2, half, half), BF16),
        vmem((2, 2, 2, half, half), BF16),
        vmem((4, extent, extent), BF16),
        vmem((4, extent, extent), BF16),
        pltpu.SMEM((1, slots, 2), jnp.int32),
        pltpu.SMEM((1, 1), jnp.int32),
        pltpu.SMEM((5, 4), jnp.int32),
        vmem((2, modes, extent, extent), F32),
        vmem((2, half, extent), F32),
        vmem((2, 2, extent, half), F32),
        vmem((2, 5, 3 * extent, half), F32),
        vmem((5, 3 * extent, half), F32),
        vmem((2, 4, big, half), F32),
        vmem((4, big, half), F32),
        vmem((2, 4, half, half), BF16),
        vmem((2, 4, half, half), BF16),
        vmem((2, extent, half), BF16),
        vmem((2, extent, half), BF16),
        vmem((2, 2, 4, half, half), BF16),
        vmem((2, 2, 4, half, half), BF16),
        vmem((2, 2, extent, half), BF16),
        vmem((2, 2, extent, half), BF16),
        pltpu.SemaphoreType.DMA((4,)),
        pltpu.SemaphoreType.DMA((COPIES,)),
        pltpu.SemaphoreType.DMA((COPIES,)),
    ]
    update = pl.pallas_call(
        functools.partial(kernel, n_row, n_col, slots, modes),
        out_shape=jax.ShapeDtypeStruct((4 * extent, half), F32),
        in_specs=[anywhere] * 4 + [pl.BlockSpec(memory_space=pltpu.SMEM)] * 2,
        out_specs=pl.BlockSpec(memory_space=pltpu.VMEM),
        scratch_shapes=scratch,
        compiler_params=pltpu.CompilerParams(
            collective_id=0, has_side_effects=True, vmem_limit_bytes=56 * 1024 * 1024
        ),
        cost_estimate=pl.CostEstimate(flops=5 * 10**9, bytes_accessed=5 * 10**6, transcendentals=3 * 10**5),
    )(obj, probe, amplitudes[0], tab, positions, counts)
    return update.reshape(extent, 2, 2, half).transpose(0, 2, 1, 3).reshape(extent, 2, extent)


def solution(mesh):
    in_specs = (
        P("row", None, "col"),
        P(),
        P("row", "col", None, None),
        P("row", "col", None),
        P("row", "col"),
    )
    out_specs = P("row", None, "col")
    step = functools.partial(on_device, mesh.shape["row"], mesh.shape["col"])
    return jax.shard_map(step, mesh=mesh, in_specs=in_specs, out_specs=out_specs, check_vma=False)
```

```python
import functools

import jax
import jax.numpy as jnp
import numpy as np
from jax import lax
from jax.experimental import pallas as pl
from jax.experimental.pallas import tpu as pltpu
from jax.sharding import PartitionSpec as P

MESH = pl.DeviceIdType.MESH
F32 = jnp.float32
BF16 = jnp.bfloat16

floor_amplitude = 0.25
ridge_weight = 1.0

POS, CNT = 0, 1
OBJ = 2
CORNER = 8
AMP = 12
WEIGHT = 16
GRAD = 24
COPIES = 32
RIGHT, LEFT = (0, 1), (0, -1)


def tables(extent):
    half = extent // 2
    steps = np.arange(extent)
    turns = np.outer(np.arange(half), steps) % extent
    scale = 1.0 / np.sqrt(extent)
    cosine = np.cos(2.0 * np.pi * turns / extent) * scale
    sine = np.sin(2.0 * np.pi * turns / extent) * scale
    forward = []
    for parity in range(2):
        c, s = cosine[:, parity::2], sine[:, parity::2]
        forward.append(np.block([[c, -s], [s, c]]))
    order = np.concatenate([steps[0::2], steps[1::2]])
    permute = np.eye(extent)[order]
    stack = [forward[0], forward[1], forward[0].T, forward[1].T, permute, permute.T]
    return np.stack(stack).astype(np.float32).astype(jnp.bfloat16)


def dot(a, b):
    return jnp.dot(a, b, preferred_element_type=F32)


def kernel(
    n_row, n_col, slots, modes,
    obj_hbm, probe_hbm, amp_hbm, tab_hbm, pos, cnt, out,
    obj, probe, amps, tab, pp, light, ext, win,
    rim, sa, ra, left_pos, left_cnt, table,
    far, fac, grad, pg, pw, cv, cw,
    ws, wi, wx, wd, wo, gs, gi, gx, gd, go,
    lsem, ssem, rsem,
):
    row, col = lax.axis_index("row"), lax.axis_index("col")
    core = lax.rem(row, 2)
    outer, inner = 2 * core - 1, 1 - 2 * core
    has = {
        "right": col < n_col - 1, "left": col > 0,
        "outer": jnp.where(core == 0, row > 0, row < n_row - 1), "inner": row >= 0,
    }
    sides = (("right", 1), ("left", -1))

    def to(vertical, across):
        step = {"outer": outer, "inner": inner, "": 0}[vertical]
        return (row + step, col + {"right": 1, "left": -1, "": 0}[across])

    def exists(vertical, across):
        if vertical and across:
            return has[vertical] & has[across]
        return has[vertical or across]

    def opposite(across):
        return {"right": "left", "left": "right", "": ""}[across]

    def remote(number, src, dst, vertical, across):
        return pltpu.make_async_remote_copy(
            src_ref=src, dst_ref=dst, send_sem=ssem.at[number], recv_sem=rsem.at[number],
            device_id=to(vertical, across), device_id_type=MESH,
        )

    sent = {}

    def send(number, src, dst, vertical, across):
        copy = remote(number, src, dst, vertical, across)
        pl.when(exists(vertical, across))(copy.start)
        sent[number] = (copy, vertical, across)

    def arrived(number):
        copy, vertical, across = sent[number]
        pl.when(exists(vertical, opposite(across)))(copy.wait_recv)

    def rows(start):
        return pl.ds(pl.multiple_of(start, 128), 128)

    outer_half, inner_half = rows(128 + 128 * core), rows(256 - 128 * core)
    outer_rim, inner_rim = rows(384 * core), rows(384 - 384 * core)

    local = [
        pltpu.make_async_copy(obj_hbm, obj, lsem.at[0]),
        pltpu.make_async_copy(amp_hbm, amps.at[pl.ds(0, slots)], lsem.at[1]),
        pltpu.make_async_copy(probe_hbm, probe, lsem.at[2]),
        pltpu.make_async_copy(tab_hbm, tab, lsem.at[3]),
    ]
    for copy in local:
        copy.start()

    barrier = pltpu.get_barrier_semaphore()
    for vertical, across in (("", "right"), ("", "left"), ("outer", ""), ("inner", "")):
        pl.when(exists(vertical, across))(
            functools.partial(
                pl.semaphore_signal, barrier, inc=1, device_id=to(vertical, across), device_id_type=MESH
            )
        )

    for c in range(2):
        for b in (0, 3):
            ext[c, b] = jnp.zeros((512, 128), F32)
        for b in (1, 2):
            ext[c, b, 0:128, :] = jnp.zeros((128, 128), F32)
            ext[c, b, 384:512, :] = jnp.zeros((128, 128), F32)
    local[0].wait()
    for c in range(2):
        for b in range(2):
            plane = obj[pl.ds(2 * b + c, 256, stride=4), :]
            ext[c, 1 + b, 128:384, :] = plane
            rim[c, 1 + b, 128:384, :] = plane.astype(BF16)

    neighbours = jnp.int32(1)
    for name in ("right", "left", "outer"):
        neighbours = neighbours + jnp.where(has[name], 1, 0)
    pl.semaphore_wait(barrier, neighbours)

    send(POS, pos, left_pos, "", "right")
    send(CNT, cnt, left_cnt, "", "right")
    for n, half in enumerate((outer_half, inner_half)):
        send(OBJ + 2 * n, rim.at[:, 2, half], rim.at[:, 0, half], "", "right")
        send(OBJ + 2 * n + 1, rim.at[:, 1, half], rim.at[:, 3, half], "", "left")
    send(OBJ + 4, rim.at[:, pl.ds(1, 2), outer_half], rim.at[:, pl.ds(1, 2), inner_rim], "outer", "")
    send(OBJ + 5, rim.at[:, pl.ds(1, 2), inner_half], rim.at[:, pl.ds(1, 2), outer_rim], "inner", "")

    def widen(number, blocks, span):
        copy, vertical, across = sent[number]

        @pl.when(exists(vertical, opposite(across)))
        def _():
            copy.wait_recv()
            for c in range(2):
                for b in blocks:
                    ext[c, b, span, :] = rim[c, b, span, :].astype(F32)

    def corners(n, half, beyond, vertical):
        for m, (side, block) in enumerate((("left", 0), ("right", 3))):
            widen(OBJ + 2 * n + m, [block], half)
            copy = remote(CORNER + 2 * n + m, rim.at[:, block, half], rim.at[:, block, beyond], vertical, "")
            there = exists(vertical, side)
            pl.when(there)(copy.start)
            corner_copies.append((copy, there, block, vertical))

    corner_copies = []

    local[1].wait()
    local[3].wait()

    def reorder(i, carry):
        amps[i] = dot(dot(tab[4], amps[i]).astype(BF16), tab[5]).astype(BF16)
        return carry

    lax.fori_loop(0, slots, reorder, 0)

    def ranked(ref, count, tile):
        rank = jnp.int32(0)
        picked = [[jnp.int32(0)] * 3 for _ in range(4)]
        for i in range(slots):
            y, x = ref[0, 0, i], ref[0, 1, i]
            here = jnp.where((i < count) & ((x >> 8) == tile), 1, 0)
            for j in range(4):
                hit = jnp.where(rank == j, here, 0)
                picked[j] = [old + hit * new for old, new in zip(picked[j], (i, y, x))]
            rank = rank + here
        return picked, rank

    going, _ = ranked(pos, cnt[0, 0], col + 1)
    for j in range(4):
        sa[j] = amps[going[j][0] & (slots - 1)]
    for j in range(4):
        send(AMP + j, sa.at[j], ra.at[j], "", "right")
    corners(0, outer_half, inner_rim, "outer")

    local[2].wait()
    for k in range(modes):
        for c in range(2):
            for b in range(2):
                pp[k, c, b] = probe[pl.ds(k * 1024 + 2 * b + c, 256, stride=4), :]
    for b in range(2):
        for first in range(0, 256, 32):
            total = None
            for k in range(modes):
                for c in range(2):
                    part = pp[k, c, b, first : first + 32, :]
                    total = part * part if total is None else total + part * part
            light[b, first : first + 32, :] = total

    pg[...] = jnp.zeros_like(pg)
    pw[...] = jnp.zeros_like(pw)
    cv[...] = jnp.zeros_like(cv)
    cw[...] = jnp.zeros_like(cw)
    for j in range(4):
        amps[slots + j] = jnp.zeros((256, 256), BF16)

    for side in range(2):

        @pl.when(jnp.logical_not(has[("left", "right")[side]]))
        def _(side=side):
            for ref in (wx, gx):
                ref[:, side] = jnp.zeros(ref.shape[:1] + ref.shape[2:], BF16)

        @pl.when(jnp.logical_not(exists("outer", ("left", "right")[side])))
        def _(side=side):
            for ref in (wd, gd):
                ref[side] = jnp.zeros(ref.shape[1:], BF16)

    @pl.when(jnp.logical_not(has["outer"]))
    def _():
        for ref in (wo, go):
            ref[...] = jnp.zeros(ref.shape, BF16)

    corners(1, inner_half, outer_rim, "inner")

    arrived(POS)
    arrived(CNT)

    @pl.when(jnp.logical_not(has["left"]))
    def _():
        left_cnt[0, 0] = 0
        for i in range(slots):
            for axis in range(2):
                left_pos[0, axis, i] = 0

    home, n_home = ranked(pos, cnt[0, 0], col)
    came, _ = ranked(left_pos, left_cnt[0, 0], col)
    for j in range(4):
        for i in range(2):
            table[3 + i, j] = came[j][1 + i]
    for j in range(4):
        from_left = j >= n_home
        there = jnp.clip(j - n_home, 0, 3)
        table[0, j] = jnp.where(from_left, slots + there, home[j][0])
        for i in range(2):
            table[1 + i, j] = jnp.where(from_left, table[3 + i, there], home[j][1 + i]) & 255

    lanes = lax.broadcasted_iota(jnp.int32, (256, 128), 1)

    def spread(ref, pieces, shift):
        keep = lanes >= shift
        low, high = (pltpu.roll(piece, shift, 1) for piece in pieces)
        ref[1, 256:512, :] = jnp.where(keep, low, 0.0)
        ref[2, 256:512, :] = jnp.where(keep, high, low)
        ref[3, 256:512, :] = jnp.where(keep, 0.0, high)

    def place(canvas, ref, y, block):
        for b in range(4):
            canvas[b] += ref[b - block + 1, pl.ds(256 - y, 512), :]

    def weigh(j, carry):
        y, x = table[1, j], table[2, j]
        spread(pw, [light[0], light[1]], x & 127)
        place(cw.at[0], pw, y, x >> 7)
        return carry

    lax.fori_loop(0, 4, weigh, 0)
    widen(OBJ + 4, [1, 2], outer_rim)
    widen(OBJ + 5, [1, 2], inner_rim)
    for copy, there, block, vertical in corner_copies:
        span = outer_rim if vertical == "outer" else inner_rim

        @pl.when(there)
        def _(copy=copy, block=block, span=span):
            copy.wait_recv()
            for c in range(2):
                ext[c, block, span, :] = rim[c, block, span, :].astype(F32)

    def halo_out(base, canvas, stage, from_inner, from_x, from_corner, from_outer):
        layers = canvas.shape[0]

        def rounded(blocks, span):
            for c in range(layers):
                for b in blocks:
                    stage[c, b, span, :] = canvas[c, b, span, :].astype(BF16)

        rounded(range(4), inner_rim)
        send(base, stage.at[:, :, inner_rim], from_inner, "inner", "")
        rounded((0, 3), outer_half)
        for n, (side, block) in enumerate((("right", 3), ("left", 0))):
            send(base + 1 + n, stage.at[:, block, outer_half], from_x.at[0, n], "", side)
        rounded(range(4), outer_rim)
        for n, (side, block) in enumerate((("right", 3), ("left", 0))):
            send(base + 3 + n, stage.at[:, block, outer_rim], from_corner.at[n], "outer", side)
        send(base + 5, stage.at[:, pl.ds(1, 2), outer_rim], from_outer, "outer", "")

    def halo_inner(base, canvas, stage, from_inner, from_x):
        arrived(base)
        for n, (side, block) in enumerate((("right", 3), ("left", 0))):
            for c in range(canvas.shape[0]):
                total = canvas[c, block, inner_half, :] + from_inner[c, block].astype(F32)
                stage[c, block, inner_half, :] = total.astype(BF16)
            send(base + 6 + n, stage.at[:, block, inner_half], from_x.at[1, n], "", side)

    halo_out(WEIGHT, cw, ws, wi, wx, wd, wo)

    def slot(j, carry):
        y, x = table[1, j], table[2, j]
        block, shift = x >> 7, x & 127
        keep = lanes >= shift
        for c in range(2):
            for b in range(2):
                near = ext[c, block + b, pl.ds(y, 256), :]
                far_off = ext[c, block + b + 1, pl.ds(y, 256), :]
                win[c, b] = pltpu.roll(jnp.where(keep, near, far_off), (128 - shift) & 127, 1)
        for k in range(modes):
            waves = []
            for b in range(2):
                p_re, p_im, w_re, w_im = pp[k, 0, b], pp[k, 1, b], win[0, b], win[1, b]
                waves.append((p_re * w_re - p_im * w_im, p_re * w_im + p_im * w_re))
            (lo_re, lo_im), (hi_re, hi_im) = waves
            even = jnp.concatenate([lo_re + hi_re, lo_im + hi_im], axis=1).astype(BF16)
            odd = jnp.concatenate([lo_re - hi_re, lo_im - hi_im], axis=1).astype(BF16)
            h_even, h_odd = dot(even, tab[0]), dot(odd, tab[1])
            for parity in range(2):
                if parity == 0:
                    e, o = h_even[:128] + h_even[128:], h_odd[:128] + h_odd[128:]
                else:
                    e, o = h_even[:128] - h_even[128:], h_odd[:128] - h_odd[128:]
                stacked = jnp.concatenate(
                    [
                        jnp.concatenate([e[:, :128], o[:, :128]], axis=1),
                        jnp.concatenate([e[:, 128:], o[:, 128:]], axis=1),
                    ],
                    axis=0,
                ).astype(BF16)
                far[parity, k] = dot(tab[2 + parity], stacked)

        @pl.when(has["left"])
        def _():
            remote(AMP + j, sa.at[j], ra.at[j], "", "right").wait_recv()
            amps[slots + j] = ra[j]

        amplitude = amps.at[table[0, j]]
        for parity in range(2):
            intensity = None
            for k in range(modes):
                re, im = far[parity, k, :128, :], far[parity, k, 128:, :]
                term = re * re + im * im
                intensity = term if intensity is None else intensity + term
            held = lax.rsqrt(jnp.maximum(intensity, floor_amplitude * floor_amplitude))
            fac[parity] = 1.0 - amplitude[128 * parity : 128 * parity + 128, :].astype(F32) * held

        for k in range(modes):
            parts = []
            for parity in range(2):
                factor = jnp.concatenate([fac[parity], fac[parity]], axis=0)
                parts.append(dot(tab[parity], (far[parity, k] * factor).astype(BF16)))
            low, high = parts[0] + parts[1], parts[0] - parts[1]
            ends = []
            for parity in range(2):
                cut = slice(128 * parity, 128 * parity + 128)
                near = jnp.concatenate(
                    [
                        jnp.concatenate([low[:128, cut], low[128:, cut]], axis=1),
                        jnp.concatenate([high[:128, cut], high[128:, cut]], axis=1),
                    ],
                    axis=0,
                ).astype(BF16)
                ends.append(dot(near, tab[2 + parity]))
            for b in range(2):
                back = ends[0] + ends[1] if b == 0 else ends[0] - ends[1]
                b_re, b_im = back[:, :128], back[:, 128:]
                p_re, p_im = pp[k, 0, b], pp[k, 1, b]
                g_re, g_im = p_re * b_re + p_im * b_im, p_re * b_im - p_im * b_re
                if k == 0:
                    grad[0, b], grad[1, b] = g_re, g_im
                else:
                    grad[0, b] += g_re
                    grad[1, b] += g_im
        for c in range(2):
            spread(pg.at[c], [grad[c, 0], grad[c, 1]], shift)
            place(cv.at[c], pg.at[c], y, block)
        return carry

    lax.fori_loop(0, 4, slot, 0)

    halo_out(GRAD, cv, gs, gi, gx, gd, go)
    halo_inner(WEIGHT, cw, ws, wi, wx)
    halo_inner(GRAD, cv, gs, gi, gx)

    def whole(canvas, c, b, from_inner, from_x, from_corner, from_outer):
        total = canvas[c, 1 + b, outer_half, :] + from_outer[c, b].astype(F32)
        total = total + from_x[0, b, c].astype(F32) + from_corner[b, c].astype(F32)
        other = canvas[c, 1 + b, inner_half, :] + from_inner[c, 1 + b].astype(F32)
        return total, other + from_x[1, b, c].astype(F32)

    for number in range(1, 8):
        arrived(WEIGHT + number)
    for b in range(2):
        far_half, near_half = whole(cw, 0, b, wi, wx, wd, wo)
        cw[0, 1 + b, outer_half, :] = 1.0 / (far_half + ridge_weight)
        cw[0, 1 + b, inner_half, :] = 1.0 / (near_half + ridge_weight)
    for number in range(1, 8):
        arrived(GRAD + number)
    for c in range(2):
        for b in range(2):
            far_half, near_half = whole(cv, c, b, gi, gx, gd, go)
            first, second = 512 * core + 2 * b + c, 512 - 512 * core + 2 * b + c
            out[pl.ds(first, 128, stride=4), :] = far_half * cw[0, 1 + b, outer_half, :]
            out[pl.ds(second, 128, stride=4), :] = near_half * cw[0, 1 + b, inner_half, :]

    for copy, vertical, across in sent.values():
        pl.when(exists(vertical, across))(copy.wait_send)
    for copy, there, _, _ in corner_copies:
        pl.when(there)(copy.wait_send)


def on_device(n_row, n_col, object_field, probe_modes, amplitudes, positions, counts):
    modes, extent = probe_modes.shape[0], probe_modes.shape[1]
    slots = amplitudes.shape[1]
    half = extent // 2
    obj = object_field.reshape(extent, 2, 2, half).transpose(0, 2, 1, 3).reshape(4 * extent, half)
    probe = probe_modes.reshape(modes, extent, 2, 2, half).transpose(0, 1, 3, 2, 4)
    probe = probe.reshape(modes * 4 * extent, half)
    tab = jnp.asarray(tables(extent))
    big = 2 * extent
    vmem, anywhere = pltpu.VMEM, pl.BlockSpec(memory_space=pl.ANY)
    scratch = [
        vmem((4 * extent, half), F32),
        vmem((modes * 4 * extent, half), F32),
        vmem((slots + 4, extent, extent), BF16),
        vmem((6, extent, extent), BF16),
        vmem((modes, 2, 2, extent, half), F32),
        vmem((2, extent, half), F32),
        vmem((2, 4, big, half), F32),
        vmem((2, 2, extent, half), F32),
        vmem((2, 4, big, half), BF16),
        vmem((4, extent, extent), BF16),
        vmem((4, extent, extent), BF16),
        pltpu.SMEM((1, 2, slots), jnp.int32),
        pltpu.SMEM((1, 1), jnp.int32),
        pltpu.SMEM((5, 4), jnp.int32),
        vmem((2, modes, extent, extent), F32),
        vmem((2, half, extent), F32),
        vmem((2, 2, extent, half), F32),
        vmem((2, 5, 3 * extent, half), F32),
        vmem((5, 3 * extent, half), F32),
        vmem((2, 4, big, half), F32),
        vmem((1, 4, big, half), F32),
        vmem((1, 4, big, half), BF16),
        vmem((1, 4, half, half), BF16),
        vmem((2, 2, 1, half, half), BF16),
        vmem((2, 1, half, half), BF16),
        vmem((1, 2, half, half), BF16),
        vmem((2, 4, big, half), BF16),
        vmem((2, 4, half, half), BF16),
        vmem((2, 2, 2, half, half), BF16),
        vmem((2, 2, half, half), BF16),
        vmem((2, 2, half, half), BF16),
        pltpu.SemaphoreType.DMA((4,)),
        pltpu.SemaphoreType.DMA((COPIES,)),
        pltpu.SemaphoreType.DMA((COPIES,)),
    ]
    update = pl.pallas_call(
        functools.partial(kernel, n_row, n_col, slots, modes),
        out_shape=jax.ShapeDtypeStruct((4 * extent, half), F32),
        in_specs=[anywhere] * 4 + [pl.BlockSpec(memory_space=pltpu.SMEM)] * 2,
        out_specs=pl.BlockSpec(memory_space=pltpu.VMEM),
        scratch_shapes=scratch,
        compiler_params=pltpu.CompilerParams(
            collective_id=0, has_side_effects=True, vmem_limit_bytes=56 * 1024 * 1024
        ),
        cost_estimate=pl.CostEstimate(flops=5 * 10**9, bytes_accessed=5 * 10**6, transcendentals=3 * 10**5),
    )(obj, probe, amplitudes[0], tab, positions.transpose(0, 2, 1), counts)
    return update.reshape(extent, 2, 2, half).transpose(0, 2, 1, 3).reshape(extent, 2, extent)


def solution(mesh):
    in_specs = (
        P("row", None, "col"),
        P(),
        P("row", "col", None, None),
        P("row", "col", None),
        P("row", "col"),
    )
    out_specs = P("row", None, "col")
    step = functools.partial(on_device, mesh.shape["row"], mesh.shape["col"])
    return jax.shard_map(step, mesh=mesh, in_specs=in_specs, out_specs=out_specs, check_vma=False)
```

```python
import functools

import jax
import jax.numpy as jnp
import numpy as np
from jax import lax
from jax.experimental import pallas as pl
from jax.experimental.pallas import tpu as pltpu
from jax.sharding import PartitionSpec as P

MESH = pl.DeviceIdType.MESH
F32 = jnp.float32
BF16 = jnp.bfloat16

floor_amplitude = 0.25
ridge_weight = 1.0

POS, CNT = 0, 1
OBJ = 2
CORNER = 8
AMP = 12
WEIGHT = 16
GRAD = 24
COPIES = 32
RIGHT, LEFT = (0, 1), (0, -1)


def tables(extent):
    half = extent // 2
    steps = np.arange(extent)
    turns = np.outer(np.arange(half), steps) % extent
    scale = 1.0 / np.sqrt(extent)
    cosine = np.cos(2.0 * np.pi * turns / extent) * scale
    sine = np.sin(2.0 * np.pi * turns / extent) * scale
    forward = []
    for parity in range(2):
        c, s = cosine[:, parity::2], sine[:, parity::2]
        forward.append(np.block([[c, -s], [s, c]]))
    order = np.concatenate([steps[0::2], steps[1::2]])
    permute = np.eye(extent)[order]
    stack = [forward[0], forward[1], forward[0].T, forward[1].T, permute, permute.T]
    return np.stack(stack).astype(np.float32).astype(jnp.bfloat16)


def dot(a, b):
    return jnp.dot(a, b, preferred_element_type=F32)


def kernel(
    n_row, n_col, slots, modes,
    obj_hbm, probe_hbm, amp_hbm, tab_hbm, pos, cnt, out,
    obj, probe, amps, tab, pp, light, ext, win,
    rim, sa, ra, left_pos, left_cnt, table,
    far, wave, stack, grad, pg, pw, cv, cw,
    ws, wi, wx, wd, wo, gs, gi, gx, gd, go,
    lsem, ssem, rsem,
):
    row, col = lax.axis_index("row"), lax.axis_index("col")
    core = lax.rem(row, 2)
    outer, inner = 2 * core - 1, 1 - 2 * core
    has = {
        "right": col < n_col - 1, "left": col > 0,
        "outer": jnp.where(core == 0, row > 0, row < n_row - 1), "inner": row >= 0,
    }
    sides = (("right", 1), ("left", -1))

    def to(vertical, across):
        step = {"outer": outer, "inner": inner, "": 0}[vertical]
        return (row + step, col + {"right": 1, "left": -1, "": 0}[across])

    def exists(vertical, across):
        if vertical and across:
            return has[vertical] & has[across]
        return has[vertical or across]

    def opposite(across):
        return {"right": "left", "left": "right", "": ""}[across]

    def remote(number, src, dst, vertical, across):
        return pltpu.make_async_remote_copy(
            src_ref=src, dst_ref=dst, send_sem=ssem.at[number], recv_sem=rsem.at[number],
            device_id=to(vertical, across), device_id_type=MESH,
        )

    sent = {}

    def send(number, src, dst, vertical, across):
        copy = remote(number, src, dst, vertical, across)
        pl.when(exists(vertical, across))(copy.start)
        sent[number] = (copy, vertical, across)

    def arrived(number):
        copy, vertical, across = sent[number]
        pl.when(exists(vertical, opposite(across)))(copy.wait_recv)

    def rows(start):
        return pl.ds(pl.multiple_of(start, 128), 128)

    outer_half, inner_half = rows(128 + 128 * core), rows(256 - 128 * core)
    outer_rim, inner_rim = rows(384 * core), rows(384 - 384 * core)

    local = [
        pltpu.make_async_copy(obj_hbm, obj, lsem.at[0]),
        pltpu.make_async_copy(amp_hbm, amps.at[pl.ds(0, slots)], lsem.at[1]),
        pltpu.make_async_copy(probe_hbm, probe, lsem.at[2]),
        pltpu.make_async_copy(tab_hbm, tab, lsem.at[3]),
    ]
    for copy in local:
        copy.start()

    barrier = pltpu.get_barrier_semaphore()
    for vertical, across in (("", "right"), ("", "left"), ("outer", ""), ("inner", "")):
        pl.when(exists(vertical, across))(
            functools.partial(
                pl.semaphore_signal, barrier, inc=1, device_id=to(vertical, across), device_id_type=MESH
            )
        )

    for c in range(2):
        for b in (0, 3):
            ext[c, b] = jnp.zeros((512, 128), F32)
        for b in (1, 2):
            ext[c, b, 0:128, :] = jnp.zeros((128, 128), F32)
            ext[c, b, 384:512, :] = jnp.zeros((128, 128), F32)
    local[0].wait()
    for c in range(2):
        for b in range(2):
            plane = obj[pl.ds(2 * b + c, 256, stride=4), :]
            ext[c, 1 + b, 128:384, :] = plane
            rim[c, 1 + b, 128:384, :] = plane.astype(BF16)

    neighbours = jnp.int32(1)
    for name in ("right", "left", "outer"):
        neighbours = neighbours + jnp.where(has[name], 1, 0)
    pl.semaphore_wait(barrier, neighbours)

    send(POS, pos, left_pos, "", "right")
    send(CNT, cnt, left_cnt, "", "right")
    for n, half in enumerate((outer_half, inner_half)):
        send(OBJ + 2 * n, rim.at[:, 2, half], rim.at[:, 0, half], "", "right")
        send(OBJ + 2 * n + 1, rim.at[:, 1, half], rim.at[:, 3, half], "", "left")
    send(OBJ + 4, rim.at[:, pl.ds(1, 2), outer_half], rim.at[:, pl.ds(1, 2), inner_rim], "outer", "")
    send(OBJ + 5, rim.at[:, pl.ds(1, 2), inner_half], rim.at[:, pl.ds(1, 2), outer_rim], "inner", "")

    def widen(number, blocks, span):
        copy, vertical, across = sent[number]

        @pl.when(exists(vertical, opposite(across)))
        def _():
            copy.wait_recv()
            for c in range(2):
                for b in blocks:
                    ext[c, b, span, :] = rim[c, b, span, :].astype(F32)

    def corners(n, half, beyond, vertical):
        for m, (side, block) in enumerate((("left", 0), ("right", 3))):
            widen(OBJ + 2 * n + m, [block], half)
            copy = remote(CORNER + 2 * n + m, rim.at[:, block, half], rim.at[:, block, beyond], vertical, "")
            there = exists(vertical, side)
            pl.when(there)(copy.start)
            corner_copies.append((copy, there, block, vertical))

    corner_copies = []

    local[1].wait()
    local[3].wait()

    def reorder(i, carry):
        amps[i] = dot(dot(tab[4], amps[i]).astype(BF16), tab[5]).astype(BF16)
        return carry

    lax.fori_loop(0, slots, reorder, 0)

    def ranked(ref, count, tile):
        rank = jnp.int32(0)
        picked = [[jnp.int32(0)] * 3 for _ in range(4)]
        for i in range(slots):
            y, x = ref[0, 0, i], ref[0, 1, i]
            here = jnp.where((i < count) & ((x >> 8) == tile), 1, 0)
            for j in range(4):
                hit = jnp.where(rank == j, here, 0)
                picked[j] = [old + hit * new for old, new in zip(picked[j], (i, y, x))]
            rank = rank + here
        return picked, rank

    going, _ = ranked(pos, cnt[0, 0], col + 1)
    for j in range(4):
        sa[j] = amps[going[j][0] & (slots - 1)]
    for j in range(4):
        send(AMP + j, sa.at[j], ra.at[j], "", "right")
    corners(0, outer_half, inner_rim, "outer")

    local[2].wait()
    for k in range(modes):
        for c in range(2):
            for b in range(2):
                pp[k, c, b] = probe[pl.ds(k * 1024 + 2 * b + c, 256, stride=4), :]
    for b in range(2):
        for first in range(0, 256, 32):
            total = None
            for k in range(modes):
                for c in range(2):
                    part = pp[k, c, b, first : first + 32, :]
                    total = part * part if total is None else total + part * part
            light[b, first : first + 32, :] = total

    for c in range(2):
        pg[c, 12] = jnp.zeros((768, 128), F32)
        for n in range(12):
            for first in (0, 512):
                pg[c, n, first : first + 256, :] = jnp.zeros((256, 128), F32)
    pw[...] = jnp.zeros_like(pw)
    cw[...] = jnp.zeros_like(cw)
    for j in range(4):
        amps[slots + j] = jnp.zeros((256, 256), BF16)

    for side in range(2):

        @pl.when(jnp.logical_not(has[("left", "right")[side]]))
        def _(side=side):
            for ref in (wx, gx):
                ref[:, side] = jnp.zeros(ref.shape[:1] + ref.shape[2:], BF16)

        @pl.when(jnp.logical_not(exists("outer", ("left", "right")[side])))
        def _(side=side):
            for ref in (wd, gd):
                ref[side] = jnp.zeros(ref.shape[1:], BF16)

    @pl.when(jnp.logical_not(has["outer"]))
    def _():
        for ref in (wo, go):
            ref[...] = jnp.zeros(ref.shape, BF16)

    corners(1, inner_half, outer_rim, "inner")

    arrived(POS)
    arrived(CNT)

    @pl.when(jnp.logical_not(has["left"]))
    def _():
        left_cnt[0, 0] = 0
        for i in range(slots):
            for axis in range(2):
                left_pos[0, axis, i] = 0

    home, n_home = ranked(pos, cnt[0, 0], col)
    came, _ = ranked(left_pos, left_cnt[0, 0], col)
    for j in range(4):
        for i in range(2):
            table[3 + i, j] = came[j][1 + i]
    for j in range(4):
        from_left = j >= n_home
        there = jnp.clip(j - n_home, 0, 3)
        table[0, j] = jnp.where(from_left, slots + there, home[j][0])
        for i in range(2):
            table[1 + i, j] = jnp.where(from_left, table[3 + i, there], home[j][1 + i]) & 255

    lanes = lax.broadcasted_iota(jnp.int32, (256, 128), 1)

    def spread(ref, pieces, shift):
        keep = lanes >= shift
        low, high = (pltpu.roll(piece, shift, 1) for piece in pieces)
        ref[1, 256:512, :] = jnp.where(keep, low, 0.0)
        ref[2, 256:512, :] = jnp.where(keep, high, low)
        ref[3, 256:512, :] = jnp.where(keep, 0.0, high)

    def place(canvas, ref, y, block):
        for b in range(4):
            canvas[b] += ref[b - block + 1, pl.ds(256 - y, 512), :]

    def weigh(j, carry):
        y, x = table[1, j], table[2, j]
        spread(pw, [light[0], light[1]], x & 127)
        place(cw.at[0], pw, y, x >> 7)
        return carry

    lax.fori_loop(0, 4, weigh, 0)
    widen(OBJ + 4, [1, 2], outer_rim)
    widen(OBJ + 5, [1, 2], inner_rim)
    for copy, there, block, vertical in corner_copies:
        span = outer_rim if vertical == "outer" else inner_rim

        @pl.when(there)
        def _(copy=copy, block=block, span=span):
            copy.wait_recv()
            for c in range(2):
                ext[c, block, span, :] = rim[c, block, span, :].astype(F32)

    def halo_out(base, gather, layers, stage, from_inner, from_x, from_corner, from_outer):
        def rounded(blocks, span):
            for c in range(layers):
                for b in blocks:
                    stage[c, b, span, :] = gather(c, b, span).astype(BF16)

        rounded(range(4), inner_rim)
        send(base, stage.at[:, :, inner_rim], from_inner, "inner", "")
        rounded((0, 3), outer_half)
        for n, (side, block) in enumerate((("right", 3), ("left", 0))):
            send(base + 1 + n, stage.at[:, block, outer_half], from_x.at[0, n], "", side)
        rounded(range(4), outer_rim)
        for n, (side, block) in enumerate((("right", 3), ("left", 0))):
            send(base + 3 + n, stage.at[:, block, outer_rim], from_corner.at[n], "outer", side)
        send(base + 5, stage.at[:, pl.ds(1, 2), outer_rim], from_outer, "outer", "")

    def halo_inner(base, gather, layers, stage, from_inner, from_x):
        arrived(base)
        for n, (side, block) in enumerate((("right", 3), ("left", 0))):
            for c in range(layers):
                total = gather(c, block, inner_half) + from_inner[c, block].astype(F32)
                stage[c, block, inner_half, :] = total.astype(BF16)
            send(base + 6 + n, stage.at[:, block, inner_half], from_x.at[1, n], "", side)

    def weight_at(c, b, span):
        return cw[c, b, span, :]

    halo_out(WEIGHT, weight_at, 1, ws, wi, wx, wd, wo)

    def cut_window(j):
        y, x = table[1, j], table[2, j]
        block, shift = x >> 7, x & 127
        keep = lax.broadcasted_iota(jnp.int32, (64, 128), 1) >= shift
        for c in range(2):
            for b in range(2):
                for first in range(0, 256, 64):
                    near = ext[c, block + b, pl.ds(y + first, 64), :]
                    beyond = ext[c, block + b + 1, pl.ds(y + first, 64), :]
                    win[c, b, first : first + 64, :] = pltpu.roll(
                        jnp.where(keep, near, beyond), (128 - shift) & 127, 1
                    )

    group = 4

    def exit_waves():
        for first in range(0, 256, 16):
            cut = slice(first, first + 16)
            at = 2 * first if first < 128 else 2 * (first - 128) + 16
            w_re = [win[0, b, cut, :] for b in range(2)]
            w_im = [win[1, b, cut, :] for b in range(2)]
            for k in range(modes):
                waves = []
                for b in range(2):
                    p_re, p_im = pp[k, 0, b, cut, :], pp[k, 1, b, cut, :]
                    waves.append((p_re * w_re[b] - p_im * w_im[b], p_re * w_im[b] + p_im * w_re[b]))
                to_rows = slice(256 * k + at, 256 * k + at + 16)
                for part in range(2):
                    low, high = waves[0][part], waves[1][part]
                    lanes_of = slice(128 * part, 128 * part + 128)
                    wave[0, to_rows, lanes_of] = (low + high).astype(BF16)
                    wave[1, to_rows, lanes_of] = (low - high).astype(BF16)

    def half_done():
        for parity in range(2):
            lanes_of = slice(128 * parity, 128 * parity + 128)
            for k in range(0, modes, group):
                done = dot(wave[parity, 256 * k : 256 * (k + group), :], tab[parity])
                for m in range(group):
                    for first in range(0, 128, 16):
                        at = 256 * m + 2 * first
                        low, high = done[at : at + 16], done[at + 16 : at + 32]
                        plus, minus = (low + high).astype(BF16), (low - high).astype(BF16)
                        for part in range(2):
                            to_rows = slice(128 * part + first, 128 * part + first + 16)
                            source = slice(128 * part, 128 * part + 128)
                            stack[0, k + m, to_rows, lanes_of] = plus[:, source]
                            stack[1, k + m, to_rows, lanes_of] = minus[:, source]

    def far_field():
        for parity in range(2):
            for k in range(modes):
                far[parity, k] = dot(tab[2 + parity], stack[parity, k])

    def residue(parity, amplitude):
        for first in range(0, 128, 16):
            upper, lower = slice(first, first + 16), slice(128 + first, 144 + first)
            re = [far[parity, k, upper, :] for k in range(modes)]
            im = [far[parity, k, lower, :] for k in range(modes)]
            intensity = None
            for k in range(modes):
                term = re[k] * re[k] + im[k] * im[k]
                intensity = term if intensity is None else intensity + term
            held = lax.rsqrt(jnp.maximum(intensity, floor_amplitude * floor_amplitude))
            measured = amplitude[128 * parity + first : 128 * parity + first + 16, :].astype(F32)
            factor = 1.0 - measured * held
            for k in range(modes):
                stack[parity, k, upper, :] = (re[k] * factor).astype(BF16)
                stack[parity, k, lower, :] = (im[k] * factor).astype(BF16)

    def near_field():
        for k in range(modes):
            even, odd = dot(tab[0], stack[0, k]), dot(tab[1], stack[1, k])
            for first in range(0, 256, 16):
                cut = slice(first, first + 16)
                part, at = first // 128, 256 * k + first % 128
                lanes_of = slice(128 * part, 128 * part + 128)
                plus, minus = (even[cut] + odd[cut]).astype(BF16), (even[cut] - odd[cut]).astype(BF16)
                for column in range(2):
                    source = slice(128 * column, 128 * column + 128)
                    wave[column, at : at + 16, lanes_of] = plus[:, source]
                    wave[column, 128 + at : 144 + at, lanes_of] = minus[:, source]

    def back_parts():
        for parity in range(2):
            for k in range(0, modes, group):
                back = dot(wave[parity, 256 * k : 256 * (k + group), :], tab[2 + parity])
                for m in range(group):
                    far[parity, k + m] = back[256 * m : 256 * m + 256]

    def gradient():
        for first in range(0, 256, 16):
            cut = slice(first, first + 16)
            total = [None] * 4
            for k in range(modes):
                e_re, o_re = far[0, k, cut, 0:128], far[1, k, cut, 0:128]
                e_im, o_im = far[0, k, cut, 128:256], far[1, k, cut, 128:256]
                for b in range(2):
                    b_re = e_re + o_re if b == 0 else e_re - o_re
                    b_im = e_im + o_im if b == 0 else e_im - o_im
                    p_re, p_im = pp[k, 0, b, cut, :], pp[k, 1, b, cut, :]
                    for n, term in ((b, p_re * b_re + p_im * b_im), (2 + b, p_re * b_im - p_im * b_re)):
                        total[n] = term if total[n] is None else total[n] + term
            for b in range(2):
                grad[0, b, cut, :] = total[b]
                grad[1, b, cut, :] = total[2 + b]

    def keep_gradient(j):
        shift = table[2, j] & 127
        for first in range(0, 256, 64):
            cut, at = slice(first, first + 64), slice(256 + first, 320 + first)
            keep = lax.broadcasted_iota(jnp.int32, (64, 128), 1) >= shift
            for c in range(2):
                low, high = (pltpu.roll(grad[c, b, cut, :], shift, 1) for b in range(2))
                pg[c, 3 * j, at, :] = jnp.where(keep, low, 0.0)
                pg[c, 3 * j + 1, at, :] = jnp.where(keep, high, low)
                pg[c, 3 * j + 2, at, :] = jnp.where(keep, 0.0, high)

    def slot(j, carry):
        cut_window(j)
        exit_waves()
        half_done()
        far_field()

        @pl.when(has["left"])
        def _():
            remote(AMP + j, sa.at[j], ra.at[j], "", "right").wait_recv()
            amps[slots + j] = ra[j]

        amplitude = amps.at[table[0, j]]
        for parity in range(2):
            residue(parity, amplitude)
        near_field()
        back_parts()
        gradient()
        keep_gradient(j)
        return carry

    lax.fori_loop(0, 4, slot, 0)

    def gradient_at(c, b, span):
        total = None
        for j in range(4):
            y, block = table[1, j], table[2, j] >> 7
            inside = (b >= block) & (b < block + 3)
            part = pg[c, jnp.where(inside, 3 * j + b - block, 12), pl.ds(256 - y + span.start, 128), :]
            total = part if total is None else total + part
        return total

    halo_out(GRAD, gradient_at, 2, gs, gi, gx, gd, go)
    halo_inner(WEIGHT, weight_at, 1, ws, wi, wx)
    halo_inner(GRAD, gradient_at, 2, gs, gi, gx)

    def whole(gather, c, b, from_inner, from_x, from_corner, from_outer):
        total = gather(c, 1 + b, outer_half) + from_outer[c, b].astype(F32)
        total = total + from_x[0, b, c].astype(F32) + from_corner[b, c].astype(F32)
        other = gather(c, 1 + b, inner_half) + from_inner[c, 1 + b].astype(F32)
        return total, other + from_x[1, b, c].astype(F32)

    for c in range(2):
        for b in (1, 2):
            for span in (outer_half, inner_half):
                cv[c, b, span, :] = gradient_at(c, b, span)

    def own_gradient(c, b, span):
        return cv[c, b, span, :]

    for number in range(1, 8):
        arrived(WEIGHT + number)
    for b in range(2):
        far_half, near_half = whole(weight_at, 0, b, wi, wx, wd, wo)
        cw[0, 1 + b, outer_half, :] = 1.0 / (far_half + ridge_weight)
        cw[0, 1 + b, inner_half, :] = 1.0 / (near_half + ridge_weight)
    for number in range(1, 8):
        arrived(GRAD + number)
    for c in range(2):
        for b in range(2):
            far_half, near_half = whole(own_gradient, c, b, gi, gx, gd, go)
            first, second = 512 * core + 2 * b + c, 512 - 512 * core + 2 * b + c
            out[pl.ds(first, 128, stride=4), :] = far_half * cw[0, 1 + b, outer_half, :]
            out[pl.ds(second, 128, stride=4), :] = near_half * cw[0, 1 + b, inner_half, :]

    for copy, vertical, across in sent.values():
        pl.when(exists(vertical, across))(copy.wait_send)
    for copy, there, _, _ in corner_copies:
        pl.when(there)(copy.wait_send)


def on_device(n_row, n_col, object_field, probe_modes, amplitudes, positions, counts):
    modes, extent = probe_modes.shape[0], probe_modes.shape[1]
    slots = amplitudes.shape[1]
    half = extent // 2
    obj = object_field.reshape(extent, 2, 2, half).transpose(0, 2, 1, 3).reshape(4 * extent, half)
    probe = probe_modes.reshape(modes, extent, 2, 2, half).transpose(0, 1, 3, 2, 4)
    probe = probe.reshape(modes * 4 * extent, half)
    tab = jnp.asarray(tables(extent))
    big = 2 * extent
    vmem, anywhere = pltpu.VMEM, pl.BlockSpec(memory_space=pl.ANY)
    scratch = [
        vmem((4 * extent, half), F32),
        vmem((modes * 4 * extent, half), F32),
        vmem((slots + 4, extent, extent), BF16),
        vmem((6, extent, extent), BF16),
        vmem((modes, 2, 2, extent, half), F32),
        vmem((2, extent, half), F32),
        vmem((2, 4, big, half), F32),
        vmem((2, 2, extent, half), F32),
        vmem((2, 4, big, half), BF16),
        vmem((4, extent, extent), BF16),
        vmem((4, extent, extent), BF16),
        pltpu.SMEM((1, 2, slots), jnp.int32),
        pltpu.SMEM((1, 1), jnp.int32),
        pltpu.SMEM((5, 4), jnp.int32),
        vmem((2, modes, extent, extent), F32),
        vmem((2, modes * extent, extent), BF16),
        vmem((2, modes, extent, extent), BF16),
        vmem((2, 2, extent, half), F32),
        vmem((2, 13, 3 * extent, half), F32),
        vmem((5, 3 * extent, half), F32),
        vmem((2, 4, big, half), F32),
        vmem((1, 4, big, half), F32),
        vmem((1, 4, big, half), BF16),
        vmem((1, 4, half, half), BF16),
        vmem((2, 2, 1, half, half), BF16),
        vmem((2, 1, half, half), BF16),
        vmem((1, 2, half, half), BF16),
        vmem((2, 4, big, half), BF16),
        vmem((2, 4, half, half), BF16),
        vmem((2, 2, 2, half, half), BF16),
        vmem((2, 2, half, half), BF16),
        vmem((2, 2, half, half), BF16),
        pltpu.SemaphoreType.DMA((4,)),
        pltpu.SemaphoreType.DMA((COPIES,)),
        pltpu.SemaphoreType.DMA((COPIES,)),
    ]
    update = pl.pallas_call(
        functools.partial(kernel, n_row, n_col, slots, modes),
        out_shape=jax.ShapeDtypeStruct((4 * extent, half), F32),
        in_specs=[anywhere] * 4 + [pl.BlockSpec(memory_space=pltpu.SMEM)] * 2,
        out_specs=pl.BlockSpec(memory_space=pltpu.VMEM),
        scratch_shapes=scratch,
        compiler_params=pltpu.CompilerParams(
            collective_id=0, has_side_effects=True, vmem_limit_bytes=56 * 1024 * 1024
        ),
        cost_estimate=pl.CostEstimate(flops=5 * 10**9, bytes_accessed=5 * 10**6, transcendentals=3 * 10**5),
    )(obj, probe, amplitudes[0], tab, positions.transpose(0, 2, 1), counts)
    return update.reshape(extent, 2, 2, half).transpose(0, 2, 1, 3).reshape(extent, 2, extent)


def solution(mesh):
    in_specs = (
        P("row", None, "col"),
        P(),
        P("row", "col", None, None),
        P("row", "col", None),
        P("row", "col"),
    )
    out_specs = P("row", None, "col")
    step = functools.partial(on_device, mesh.shape["row"], mesh.shape["col"])
    return jax.shard_map(step, mesh=mesh, in_specs=in_specs, out_specs=out_specs, check_vma=False)
```

```python
import functools

import jax
import jax.numpy as jnp
import numpy as np
from jax import lax
from jax.experimental import pallas as pl
from jax.experimental.pallas import tpu as pltpu
from jax.sharding import PartitionSpec as P

MESH = pl.DeviceIdType.MESH
F32 = jnp.float32
BF16 = jnp.bfloat16

floor_amplitude = 0.25
ridge_weight = 1.0

POS, CNT = 0, 1
OBJ = 2
CORNER = 8
AMP = 12
WEIGHT = 16
GRAD = 24
COPIES = 32
RIGHT, LEFT = (0, 1), (0, -1)


def tables(extent):
    half = extent // 2
    steps = np.arange(extent)
    turns = np.outer(np.arange(half), steps) % extent
    scale = 1.0 / np.sqrt(extent)
    cosine = np.cos(2.0 * np.pi * turns / extent) * scale
    sine = np.sin(2.0 * np.pi * turns / extent) * scale
    forward = []
    for parity in range(2):
        c, s = cosine[:, parity::2], sine[:, parity::2]
        forward.append(np.block([[c, -s], [s, c]]))
    order = np.concatenate([steps[0::2], steps[1::2]])
    permute = np.eye(extent)[order]
    stack = [forward[0], forward[1], forward[0].T, forward[1].T, permute, permute.T]
    return np.stack(stack).astype(np.float32).astype(jnp.bfloat16)


def dot(a, b):
    return jnp.dot(a, b, preferred_element_type=F32)


def kernel(
    n_row, n_col, slots, modes,
    obj_hbm, probe_hbm, amp_hbm, tab_hbm, pos_hbm, cnt_hbm, out,
    pos, cnt, obj, probe, amps, tab, pp, light, ext, win,
    rim, sa, ra, left_pos, left_cnt, table,
    far, ends, wave, near, stack, turned, grad, pg, pw, cv, cw,
    ws, wi, wx, wd, wo, gs, gi, gx, gd, go,
    lsem, ssem, rsem,
):
    row, col = lax.axis_index("row"), lax.axis_index("col")
    core = lax.rem(row, 2)
    outer, inner = 2 * core - 1, 1 - 2 * core
    has = {
        "right": col < n_col - 1, "left": col > 0,
        "outer": jnp.where(core == 0, row > 0, row < n_row - 1), "inner": row >= 0,
    }
    sides = (("right", 1), ("left", -1))

    def to(vertical, across):
        step = {"outer": outer, "inner": inner, "": 0}[vertical]
        return (row + step, col + {"right": 1, "left": -1, "": 0}[across])

    def exists(vertical, across):
        if vertical and across:
            return has[vertical] & has[across]
        return has[vertical or across]

    def opposite(across):
        return {"right": "left", "left": "right", "": ""}[across]

    def remote(number, src, dst, vertical, across):
        return pltpu.make_async_remote_copy(
            src_ref=src, dst_ref=dst, send_sem=ssem.at[number], recv_sem=rsem.at[number],
            device_id=to(vertical, across), device_id_type=MESH,
        )

    sent = {}

    def send(number, src, dst, vertical, across):
        copy = remote(number, src, dst, vertical, across)
        pl.when(exists(vertical, across))(copy.start)
        sent[number] = (copy, vertical, across)

    def arrived(number):
        copy, vertical, across = sent[number]
        pl.when(exists(vertical, opposite(across)))(copy.wait_recv)

    def rows(start):
        return pl.ds(pl.multiple_of(start, 128), 128)

    outer_half, inner_half = rows(128 + 128 * core), rows(256 - 128 * core)
    outer_rim, inner_rim = rows(384 * core), rows(384 - 384 * core)

    local = [
        pltpu.make_async_copy(obj_hbm, obj, lsem.at[0]),
        pltpu.make_async_copy(amp_hbm, amps.at[pl.ds(0, slots)], lsem.at[1]),
        pltpu.make_async_copy(probe_hbm, probe, lsem.at[2]),
        pltpu.make_async_copy(tab_hbm, tab, lsem.at[3]),
        pltpu.make_async_copy(pos_hbm, pos, lsem.at[4]),
        pltpu.make_async_copy(cnt_hbm, cnt, lsem.at[5]),
    ]
    for n in (0, 4, 5):
        local[n].start()

    barrier = pltpu.get_barrier_semaphore()
    for vertical, across in (("", "right"), ("", "left"), ("outer", ""), ("inner", "")):
        pl.when(exists(vertical, across))(
            functools.partial(
                pl.semaphore_signal, barrier, inc=1, device_id=to(vertical, across), device_id_type=MESH
            )
        )

    for c in range(2):
        for b in (0, 3):
            ext[c, b] = jnp.zeros((512, 128), F32)
        for b in (1, 2):
            ext[c, b, 0:128, :] = jnp.zeros((128, 128), F32)
            ext[c, b, 384:512, :] = jnp.zeros((128, 128), F32)
    local[0].wait()
    for n in (1, 3, 2):
        local[n].start()
    for c in range(2):
        for b in range(2):
            plane = obj[pl.ds(2 * b + c, 256, stride=4), :]
            ext[c, 1 + b, 128:384, :] = plane
            rim[c, 1 + b, 128:384, :] = plane.astype(BF16)

    neighbours = jnp.int32(1)
    for name in ("right", "left", "outer"):
        neighbours = neighbours + jnp.where(has[name], 1, 0)
    pl.semaphore_wait(barrier, neighbours)

    local[4].wait()
    local[5].wait()
    send(POS, pos, left_pos, "", "right")
    send(CNT, cnt, left_cnt, "", "right")
    for n, half in enumerate((outer_half, inner_half)):
        send(OBJ + 2 * n, rim.at[:, 2, half], rim.at[:, 0, half], "", "right")
        send(OBJ + 2 * n + 1, rim.at[:, 1, half], rim.at[:, 3, half], "", "left")
    send(OBJ + 4, rim.at[:, pl.ds(1, 2), outer_half], rim.at[:, pl.ds(1, 2), inner_rim], "outer", "")
    send(OBJ + 5, rim.at[:, pl.ds(1, 2), inner_half], rim.at[:, pl.ds(1, 2), outer_rim], "inner", "")

    def widen(number, blocks, span):
        copy, vertical, across = sent[number]

        @pl.when(exists(vertical, opposite(across)))
        def _():
            copy.wait_recv()
            for c in range(2):
                for b in blocks:
                    ext[c, b, span, :] = rim[c, b, span, :].astype(F32)

    def corners(n, half, beyond, vertical):
        for m, (side, block) in enumerate((("left", 0), ("right", 3))):
            widen(OBJ + 2 * n + m, [block], half)
            copy = remote(CORNER + 2 * n + m, rim.at[:, block, half], rim.at[:, block, beyond], vertical, "")
            there = exists(vertical, side)
            pl.when(there)(copy.start)
            corner_copies.append((copy, there, block, vertical))

    corner_copies = []

    local[1].wait()
    local[3].wait()

    def reorder(i, carry):
        amps[i] = dot(dot(tab[4], amps[i]).astype(BF16), tab[5]).astype(BF16)
        return carry

    lax.fori_loop(0, slots, reorder, 0)

    def ranked(ref, count, tile):
        rank = jnp.int32(0)
        picked = [[jnp.int32(0)] * 3 for _ in range(4)]
        for i in range(slots):
            y, x = ref[0, 0, i], ref[0, 1, i]
            here = jnp.where((i < count) & ((x >> 8) == tile), 1, 0)
            for j in range(4):
                hit = jnp.where(rank == j, here, 0)
                picked[j] = [old + hit * new for old, new in zip(picked[j], (i, y, x))]
            rank = rank + here
        return picked, rank

    going, _ = ranked(pos, cnt[0, 0], col + 1)
    for j in range(4):
        sa[j] = amps[going[j][0] & (slots - 1)]
    for j in range(4):
        send(AMP + j, sa.at[j], ra.at[j], "", "right")
    corners(0, outer_half, inner_rim, "outer")

    local[2].wait()
    for k in range(modes):
        for c in range(2):
            for b in range(2):
                pp[k, c, b] = probe[pl.ds(k * 1024 + 2 * b + c, 256, stride=4), :]
    for b in range(2):
        for first in range(0, 256, 32):
            total = None
            for k in range(modes):
                for c in range(2):
                    part = pp[k, c, b, first : first + 32, :]
                    total = part * part if total is None else total + part * part
            light[b, first : first + 32, :] = total

    for c in range(2):
        pg[c, 12] = jnp.zeros((768, 128), F32)
        for n in range(12):
            for first in (0, 512):
                pg[c, n, first : first + 256, :] = jnp.zeros((256, 128), F32)
    pw[...] = jnp.zeros_like(pw)
    cw[...] = jnp.zeros_like(cw)
    for j in range(4):
        amps[slots + j] = jnp.zeros((256, 256), BF16)

    for side in range(2):

        @pl.when(jnp.logical_not(has[("left", "right")[side]]))
        def _(side=side):
            for ref in (wx, gx):
                ref[:, side] = jnp.zeros(ref.shape[:1] + ref.shape[2:], BF16)

        @pl.when(jnp.logical_not(exists("outer", ("left", "right")[side])))
        def _(side=side):
            for ref in (wd, gd):
                ref[side] = jnp.zeros(ref.shape[1:], BF16)

    @pl.when(jnp.logical_not(has["outer"]))
    def _():
        for ref in (wo, go):
            ref[...] = jnp.zeros(ref.shape, BF16)

    corners(1, inner_half, outer_rim, "inner")

    arrived(POS)
    arrived(CNT)

    @pl.when(jnp.logical_not(has["left"]))
    def _():
        left_cnt[0, 0] = 0
        for i in range(slots):
            for axis in range(2):
                left_pos[0, axis, i] = 0

    home, n_home = ranked(pos, cnt[0, 0], col)
    came, _ = ranked(left_pos, left_cnt[0, 0], col)
    for j in range(4):
        for i in range(2):
            table[3 + i, j] = came[j][1 + i]
    for j in range(4):
        from_left = j >= n_home
        there = jnp.clip(j - n_home, 0, 3)
        table[0, j] = jnp.where(from_left, slots + there, home[j][0])
        for i in range(2):
            table[1 + i, j] = jnp.where(from_left, table[3 + i, there], home[j][1 + i]) & 255

    lanes = lax.broadcasted_iota(jnp.int32, (256, 128), 1)

    def spread(ref, pieces, shift):
        keep = lanes >= shift
        low, high = (pltpu.roll(piece, shift, 1) for piece in pieces)
        ref[1, 256:512, :] = jnp.where(keep, low, 0.0)
        ref[2, 256:512, :] = jnp.where(keep, high, low)
        ref[3, 256:512, :] = jnp.where(keep, 0.0, high)

    def place(canvas, ref, y, block):
        for b in range(4):
            canvas[b] += ref[b - block + 1, pl.ds(256 - y, 512), :]

    def weigh(j, carry):
        y, x = table[1, j], table[2, j]
        spread(pw, [light[0], light[1]], x & 127)
        place(cw.at[0], pw, y, x >> 7)
        return carry

    lax.fori_loop(0, 4, weigh, 0)
    widen(OBJ + 4, [1, 2], outer_rim)
    widen(OBJ + 5, [1, 2], inner_rim)
    for copy, there, block, vertical in corner_copies:
        span = outer_rim if vertical == "outer" else inner_rim

        @pl.when(there)
        def _(copy=copy, block=block, span=span):
            copy.wait_recv()
            for c in range(2):
                ext[c, block, span, :] = rim[c, block, span, :].astype(F32)

    def halo_out(base, gather, layers, stage, from_inner, from_x, from_corner, from_outer):
        def rounded(blocks, span):
            for c in range(layers):
                for b in blocks:
                    stage[c, b, span, :] = gather(c, b, span).astype(BF16)

        rounded(range(4), inner_rim)
        send(base, stage.at[:, :, inner_rim], from_inner, "inner", "")
        rounded((0, 3), outer_half)
        for n, (side, block) in enumerate((("right", 3), ("left", 0))):
            send(base + 1 + n, stage.at[:, block, outer_half], from_x.at[0, n], "", side)
        rounded(range(4), outer_rim)
        for n, (side, block) in enumerate((("right", 3), ("left", 0))):
            send(base + 3 + n, stage.at[:, block, outer_rim], from_corner.at[n], "outer", side)
        send(base + 5, stage.at[:, pl.ds(1, 2), outer_rim], from_outer, "outer", "")

    def halo_inner(base, gather, layers, stage, from_inner, from_x):
        arrived(base)
        for n, (side, block) in enumerate((("right", 3), ("left", 0))):
            for c in range(layers):
                total = gather(c, block, inner_half) + from_inner[c, block].astype(F32)
                stage[c, block, inner_half, :] = total.astype(BF16)
            send(base + 6 + n, stage.at[:, block, inner_half], from_x.at[1, n], "", side)

    def weight_at(c, b, span):
        return cw[c, b, span, :]

    halo_out(WEIGHT, weight_at, 1, ws, wi, wx, wd, wo)

    def cut_window(j):
        y, x = table[1, j], table[2, j]
        block, shift = x >> 7, x & 127
        keep = lax.broadcasted_iota(jnp.int32, (64, 128), 1) >= shift
        for c in range(2):
            for b in range(2):
                for first in range(0, 256, 64):
                    near = ext[c, block + b, pl.ds(y + first, 64), :]
                    beyond = ext[c, block + b + 1, pl.ds(y + first, 64), :]
                    win[c, b, first : first + 64, :] = pltpu.roll(
                        jnp.where(keep, near, beyond), (128 - shift) & 127, 1
                    )


    def exit_waves():
        def piece(first, k):
            cut = slice(first, first + 16)
            at = 2 * first if first < 128 else 2 * (first - 128) + 16
            waves = []
            for b in range(2):
                p_re, p_im, w_re, w_im = pp[k, 0, b, cut, :], pp[k, 1, b, cut, :], win[0, b, cut, :], win[1, b, cut, :]
                waves.append((p_re * w_re - p_im * w_im, p_re * w_im + p_im * w_re))
            to_rows = slice(256 * k + at, 256 * k + at + 16)
            for part in range(2):
                low, high = waves[0][part], waves[1][part]
                lanes_of = slice(128 * part, 128 * part + 128)
                wave[0, to_rows, lanes_of] = (low + high).astype(BF16)
                wave[1, to_rows, lanes_of] = (low - high).astype(BF16)

        return [functools.partial(piece, first, k) for first in range(0, 256, 16) for k in range(modes)]

    def half_done():
        done = {}

        def product(parity):
            done[parity] = dot(wave[parity], tab[parity])

        def piece(parity, k, first):
            lanes_of = slice(128 * parity, 128 * parity + 128)
            at = 256 * k + 2 * first
            low, high = done[parity][at : at + 16], done[parity][at + 16 : at + 32]
            plus, minus = (low + high).astype(BF16), (low - high).astype(BF16)
            for part in range(2):
                to_rows = slice(128 * part + first, 128 * part + first + 16)
                source = slice(128 * part, 128 * part + 128)
                stack[0, k, to_rows, lanes_of] = plus[:, source]
                stack[1, k, to_rows, lanes_of] = minus[:, source]

        pieces = []
        for parity in range(2):
            pieces.append(functools.partial(product, parity))
            pieces += [functools.partial(piece, parity, k, f) for k in range(modes) for f in range(0, 128, 16)]
        return pieces

    def far_field():
        def piece(parity, k):
            far[parity, k] = dot(tab[2 + parity], stack[parity, k])

        return [functools.partial(piece, parity, k) for parity in range(2) for k in range(modes)]

    def residue(parity, amplitude):
        for first in range(0, 128, 16):
            upper, lower = slice(first, first + 16), slice(128 + first, 144 + first)
            re = [far[parity, k, upper, :] for k in range(modes)]
            im = [far[parity, k, lower, :] for k in range(modes)]
            intensity = None
            for k in range(modes):
                term = re[k] * re[k] + im[k] * im[k]
                intensity = term if intensity is None else intensity + term
            held = lax.rsqrt(jnp.maximum(intensity, floor_amplitude * floor_amplitude))
            measured = amplitude[128 * parity + first : 128 * parity + first + 16, :].astype(F32)
            factor = 1.0 - measured * held
            for k in range(modes):
                turned[parity, k, upper, :] = (re[k] * factor).astype(BF16)
                turned[parity, k, lower, :] = (im[k] * factor).astype(BF16)

    def near_field():
        done = {}

        def product(parity, k):
            done[parity, k] = dot(tab[parity], turned[parity, k])

        def piece(k, first):
            cut = slice(first, first + 16)
            part, at = first // 128, 256 * k + first % 128
            lanes_of = slice(128 * part, 128 * part + 128)
            even, odd = done[0, k][cut], done[1, k][cut]
            plus, minus = (even + odd).astype(BF16), (even - odd).astype(BF16)
            for column in range(2):
                source = slice(128 * column, 128 * column + 128)
                near[column, at : at + 16, lanes_of] = plus[:, source]
                near[column, 128 + at : 144 + at, lanes_of] = minus[:, source]

        pieces = []
        for k in range(modes):
            pieces += [functools.partial(product, parity, k) for parity in range(2)]
            pieces += [functools.partial(piece, k, first) for first in range(0, 256, 16)]
        return pieces

    def back_parts():
        def piece(parity):
            back = dot(near[parity], tab[2 + parity])
            for k in range(modes):
                ends[parity, k] = back[256 * k : 256 * k + 256]

        return [functools.partial(piece, parity) for parity in range(2)]

    def gradient():
        def piece(first):
            cut = slice(first, first + 16)
            total = [None] * 4
            for k in range(modes):
                e_re, o_re = ends[0, k, cut, 0:128], ends[1, k, cut, 0:128]
                e_im, o_im = ends[0, k, cut, 128:256], ends[1, k, cut, 128:256]
                for b in range(2):
                    b_re = e_re + o_re if b == 0 else e_re - o_re
                    b_im = e_im + o_im if b == 0 else e_im - o_im
                    p_re, p_im = pp[k, 0, b, cut, :], pp[k, 1, b, cut, :]
                    for n, term in ((b, p_re * b_re + p_im * b_im), (2 + b, p_re * b_im - p_im * b_re)):
                        total[n] = term if total[n] is None else total[n] + term
            for b in range(2):
                grad[0, b, cut, :] = total[b]
                grad[1, b, cut, :] = total[2 + b]

        return [functools.partial(piece, first) for first in range(0, 256, 16)]

    def take_turns(*stages):
        marked = [((n + 0.5) / len(stage), m, piece) for m, stage in enumerate(stages) for n, piece in enumerate(stage)]
        for _, _, piece in sorted(marked, key=lambda entry: entry[:2]):
            piece()

    def keep_gradient(j):
        shift = table[2, j] & 127
        for first in range(0, 256, 64):
            cut, at = slice(first, first + 64), slice(256 + first, 320 + first)
            keep = lax.broadcasted_iota(jnp.int32, (64, 128), 1) >= shift
            for c in range(2):
                low, high = (pltpu.roll(grad[c, b, cut, :], shift, 1) for b in range(2))
                pg[c, 3 * j, at, :] = jnp.where(keep, low, 0.0)
                pg[c, 3 * j + 1, at, :] = jnp.where(keep, high, low)
                pg[c, 3 * j + 2, at, :] = jnp.where(keep, 0.0, high)

    def start_window(j):
        cut_window(j)
        take_turns(exit_waves())
        take_turns(half_done())
        take_turns(far_field())

    def factor_window(j):
        @pl.when(has["left"])
        def _():
            remote(AMP + j, sa.at[j], ra.at[j], "", "right").wait_recv()
            amps[slots + j] = ra[j]

        amplitude = amps.at[table[0, j]]
        for parity in range(2):
            residue(parity, amplitude)

    def slot(j, carry):
        factor_window(j)
        cut_window(j + 1)
        take_turns(near_field(), exit_waves())
        take_turns(half_done())
        take_turns(back_parts())
        take_turns(far_field(), gradient())
        keep_gradient(j)
        return carry

    start_window(0)
    lax.fori_loop(0, 3, slot, 0)
    factor_window(3)
    for stage in (near_field, back_parts, gradient):
        take_turns(stage())
    keep_gradient(3)

    def gradient_at(c, b, span):
        total = None
        for j in range(4):
            y, block = table[1, j], table[2, j] >> 7
            inside = (b >= block) & (b < block + 3)
            part = pg[c, jnp.where(inside, 3 * j + b - block, 12), pl.ds(256 - y + span.start, 128), :]
            total = part if total is None else total + part
        return total

    halo_out(GRAD, gradient_at, 2, gs, gi, gx, gd, go)
    halo_inner(WEIGHT, weight_at, 1, ws, wi, wx)
    halo_inner(GRAD, gradient_at, 2, gs, gi, gx)

    def whole(gather, c, b, from_inner, from_x, from_corner, from_outer):
        total = gather(c, 1 + b, outer_half) + from_outer[c, b].astype(F32)
        total = total + from_x[0, b, c].astype(F32) + from_corner[b, c].astype(F32)
        other = gather(c, 1 + b, inner_half) + from_inner[c, 1 + b].astype(F32)
        return total, other + from_x[1, b, c].astype(F32)

    for c in range(2):
        for b in (1, 2):
            for span in (outer_half, inner_half):
                cv[c, b, span, :] = gradient_at(c, b, span)

    def own_gradient(c, b, span):
        return cv[c, b, span, :]

    for number in range(1, 8):
        arrived(WEIGHT + number)
    for b in range(2):
        far_half, near_half = whole(weight_at, 0, b, wi, wx, wd, wo)
        cw[0, 1 + b, outer_half, :] = 1.0 / (far_half + ridge_weight)
        cw[0, 1 + b, inner_half, :] = 1.0 / (near_half + ridge_weight)
    for number in range(1, 8):
        arrived(GRAD + number)
    for c in range(2):
        for b in range(2):
            far_half, near_half = whole(own_gradient, c, b, gi, gx, gd, go)
            first, second = 512 * core + 2 * b + c, 512 - 512 * core + 2 * b + c
            out[pl.ds(first, 128, stride=4), :] = far_half * cw[0, 1 + b, outer_half, :]
            out[pl.ds(second, 128, stride=4), :] = near_half * cw[0, 1 + b, inner_half, :]

    for copy, vertical, across in sent.values():
        pl.when(exists(vertical, across))(copy.wait_send)
    for copy, there, _, _ in corner_copies:
        pl.when(there)(copy.wait_send)


def on_device(n_row, n_col, object_field, probe_modes, amplitudes, positions, counts):
    modes, extent = probe_modes.shape[0], probe_modes.shape[1]
    slots = amplitudes.shape[1]
    half = extent // 2
    obj = object_field.reshape(extent, 2, 2, half).transpose(0, 2, 1, 3).reshape(4 * extent, half)
    probe = probe_modes.reshape(modes, extent, 2, 2, half).transpose(0, 1, 3, 2, 4)
    probe = probe.reshape(modes * 4 * extent, half)
    tab = jnp.asarray(tables(extent))
    big = 2 * extent
    vmem, anywhere = pltpu.VMEM, pl.BlockSpec(memory_space=pl.ANY)
    scratch = [
        pltpu.SMEM((1, 2, slots), jnp.int32),
        pltpu.SMEM((1, 1), jnp.int32),
        vmem((4 * extent, half), F32),
        vmem((modes * 4 * extent, half), F32),
        vmem((slots + 4, extent, extent), BF16),
        vmem((6, extent, extent), BF16),
        vmem((modes, 2, 2, extent, half), F32),
        vmem((2, extent, half), F32),
        vmem((2, 4, big, half), F32),
        vmem((2, 2, extent, half), F32),
        vmem((2, 4, big, half), BF16),
        vmem((4, extent, extent), BF16),
        vmem((4, extent, extent), BF16),
        pltpu.SMEM((1, 2, slots), jnp.int32),
        pltpu.SMEM((1, 1), jnp.int32),
        pltpu.SMEM((5, 4), jnp.int32),
        vmem((2, modes, extent, extent), F32),
        vmem((2, modes, extent, extent), F32),
        vmem((2, modes * extent, extent), BF16),
        vmem((2, modes * extent, extent), BF16),
        vmem((2, modes, extent, extent), BF16),
        vmem((2, modes, extent, extent), BF16),
        vmem((2, 2, extent, half), F32),
        vmem((2, 13, 3 * extent, half), F32),
        vmem((5, 3 * extent, half), F32),
        vmem((2, 4, big, half), F32),
        vmem((1, 4, big, half), F32),
        vmem((1, 4, big, half), BF16),
        vmem((1, 4, half, half), BF16),
        vmem((2, 2, 1, half, half), BF16),
        vmem((2, 1, half, half), BF16),
        vmem((1, 2, half, half), BF16),
        vmem((2, 4, big, half), BF16),
        vmem((2, 4, half, half), BF16),
        vmem((2, 2, 2, half, half), BF16),
        vmem((2, 2, half, half), BF16),
        vmem((2, 2, half, half), BF16),
        pltpu.SemaphoreType.DMA((6,)),
        pltpu.SemaphoreType.DMA((COPIES,)),
        pltpu.SemaphoreType.DMA((COPIES,)),
    ]
    update = pl.pallas_call(
        functools.partial(kernel, n_row, n_col, slots, modes),
        out_shape=pltpu.VMEM((4 * extent, half), F32),
        in_specs=[anywhere] * 6,
        out_specs=pl.BlockSpec(memory_space=pltpu.VMEM),
        scratch_shapes=scratch,
        compiler_params=pltpu.CompilerParams(
            collective_id=0, has_side_effects=True, vmem_limit_bytes=56 * 1024 * 1024
        ),
        cost_estimate=pl.CostEstimate(flops=5 * 10**9, bytes_accessed=5 * 10**6, transcendentals=3 * 10**5),
    )(obj, probe, amplitudes[0], tab, positions.transpose(0, 2, 1), counts)
    return update.reshape(extent, 2, 2, half).transpose(0, 2, 1, 3).reshape(extent, 2, extent)


def solution(mesh):
    in_specs = (
        P("row", None, "col"),
        P(),
        P("row", "col", None, None),
        P("row", "col", None),
        P("row", "col"),
    )
    out_specs = P("row", None, "col")
    step = functools.partial(on_device, mesh.shape["row"], mesh.shape["col"])
    return jax.shard_map(step, mesh=mesh, in_specs=in_specs, out_specs=out_specs, check_vma=False)
```

```python
import functools

import jax
import jax.numpy as jnp
import numpy as np
from jax import lax
from jax.experimental import pallas as pl
from jax.experimental.pallas import tpu as pltpu
from jax.sharding import PartitionSpec as P

MESH = pl.DeviceIdType.MESH
F32 = jnp.float32
BF16 = jnp.bfloat16

floor_amplitude = 0.25
ridge_weight = 1.0

POS, CNT = 0, 1
OBJ = 2
CORNER = 8
AMP = 12
WEIGHT = 16
GRAD = 24
COPIES = 32
RIGHT, LEFT = (0, 1), (0, -1)


def tables(extent):
    half = extent // 2
    steps = np.arange(extent)
    turns = np.outer(np.arange(half), steps) % extent
    scale = 1.0 / np.sqrt(extent)
    cosine = np.cos(2.0 * np.pi * turns / extent) * scale
    sine = np.sin(2.0 * np.pi * turns / extent) * scale
    forward = []
    for parity in range(2):
        c, s = cosine[:, parity::2], sine[:, parity::2]
        forward.append(np.block([[c, -s], [s, c]]))
    order = np.concatenate([steps[0::2], steps[1::2]])
    permute = np.eye(extent)[order]
    stack = [forward[0], forward[1], forward[0].T, forward[1].T, permute, permute.T]
    return np.stack(stack).astype(np.float32).astype(jnp.bfloat16)


def dot(a, b):
    return jnp.dot(a, b, preferred_element_type=F32)


def kernel(
    n_row, n_col, slots, modes,
    obj_hbm, probe_hbm, amp_hbm, tab_hbm, pos_hbm, cnt_hbm, out,
    pos, cnt, obj, probe, amps, held, tab, pp, light, ext, win,
    rim, sa, ra, left_pos, left_cnt, table,
    far, ends, wave, near, stack, turned, grad, pg, pw, cv, cw,
    ws, wi, wx, wd, wo, gs, gi, gx, gd, go,
    lsem, ssem, rsem,
):
    row, col = lax.axis_index("row"), lax.axis_index("col")
    core = lax.rem(row, 2)
    outer, inner = 2 * core - 1, 1 - 2 * core
    has = {
        "right": col < n_col - 1, "left": col > 0,
        "outer": jnp.where(core == 0, row > 0, row < n_row - 1), "inner": row >= 0,
    }
    sides = (("right", 1), ("left", -1))

    def to(vertical, across):
        step = {"outer": outer, "inner": inner, "": 0}[vertical]
        return (row + step, col + {"right": 1, "left": -1, "": 0}[across])

    def exists(vertical, across):
        if vertical and across:
            return has[vertical] & has[across]
        return has[vertical or across]

    def opposite(across):
        return {"right": "left", "left": "right", "": ""}[across]

    def remote(number, src, dst, vertical, across):
        return pltpu.make_async_remote_copy(
            src_ref=src, dst_ref=dst, send_sem=ssem.at[number], recv_sem=rsem.at[number],
            device_id=to(vertical, across), device_id_type=MESH,
        )

    sent = {}

    def send(number, src, dst, vertical, across):
        copy = remote(number, src, dst, vertical, across)
        pl.when(exists(vertical, across))(copy.start)
        sent[number] = (copy, vertical, across)

    def arrived(number):
        copy, vertical, across = sent[number]
        pl.when(exists(vertical, opposite(across)))(copy.wait_recv)

    def rows(start):
        return pl.ds(pl.multiple_of(start, 128), 128)

    outer_half, inner_half = rows(128 + 128 * core), rows(256 - 128 * core)
    outer_rim, inner_rim = rows(384 * core), rows(384 - 384 * core)

    local = [
        pltpu.make_async_copy(obj_hbm, obj, lsem.at[0]),
        pltpu.make_async_copy(amp_hbm, amps, lsem.at[1]),
        pltpu.make_async_copy(probe_hbm, probe, lsem.at[2]),
        pltpu.make_async_copy(tab_hbm, tab, lsem.at[3]),
        pltpu.make_async_copy(pos_hbm, pos, lsem.at[4]),
        pltpu.make_async_copy(cnt_hbm, cnt, lsem.at[5]),
    ]
    for n in (0, 4, 5):
        local[n].start()

    barrier = pltpu.get_barrier_semaphore()
    for vertical, across in (("", "right"), ("", "left"), ("outer", ""), ("inner", "")):
        pl.when(exists(vertical, across))(
            functools.partial(
                pl.semaphore_signal, barrier, inc=1, device_id=to(vertical, across), device_id_type=MESH
            )
        )

    for c in range(2):
        for b in (0, 3):
            ext[c, b] = jnp.zeros((512, 128), F32)
        for b in (1, 2):
            ext[c, b, 0:128, :] = jnp.zeros((128, 128), F32)
            ext[c, b, 384:512, :] = jnp.zeros((128, 128), F32)
    local[0].wait()
    for n in (1, 3, 2):
        local[n].start()
    for c in range(2):
        for b in range(2):
            plane = obj[pl.ds(2 * b + c, 256, stride=4), :]
            ext[c, 1 + b, 128:384, :] = plane
            rim[c, 1 + b, 128:384, :] = plane.astype(BF16)

    neighbours = jnp.int32(1)
    for name in ("right", "left", "outer"):
        neighbours = neighbours + jnp.where(has[name], 1, 0)
    pl.semaphore_wait(barrier, neighbours)

    local[4].wait()
    local[5].wait()
    send(POS, pos, left_pos, "", "right")
    send(CNT, cnt, left_cnt, "", "right")
    for n, half in enumerate((outer_half, inner_half)):
        send(OBJ + 2 * n, rim.at[:, 2, half], rim.at[:, 0, half], "", "right")
        send(OBJ + 2 * n + 1, rim.at[:, 1, half], rim.at[:, 3, half], "", "left")
    send(OBJ + 4, rim.at[:, pl.ds(1, 2), outer_half], rim.at[:, pl.ds(1, 2), inner_rim], "outer", "")
    send(OBJ + 5, rim.at[:, pl.ds(1, 2), inner_half], rim.at[:, pl.ds(1, 2), outer_rim], "inner", "")

    def widen(number, blocks, span):
        copy, vertical, across = sent[number]

        @pl.when(exists(vertical, opposite(across)))
        def _():
            copy.wait_recv()
            for c in range(2):
                for b in blocks:
                    ext[c, b, span, :] = rim[c, b, span, :].astype(F32)

    def corners(n, half, beyond, vertical):
        for m, (side, block) in enumerate((("left", 0), ("right", 3))):
            widen(OBJ + 2 * n + m, [block], half)
            copy = remote(CORNER + 2 * n + m, rim.at[:, block, half], rim.at[:, block, beyond], vertical, "")
            there = exists(vertical, side)
            pl.when(there)(copy.start)
            corner_copies.append((copy, there, block, vertical))

    corner_copies = []

    def ranked(ref, count, tile):
        rank = jnp.int32(0)
        picked = [[jnp.int32(0)] * 3 for _ in range(4)]
        for i in range(slots):
            y, x = ref[0, 0, i], ref[0, 1, i]
            here = jnp.where((i < count) & ((x >> 8) == tile), 1, 0)
            for j in range(4):
                hit = jnp.where(rank == j, here, 0)
                picked[j] = [old + hit * new for old, new in zip(picked[j], (i, y, x))]
            rank = rank + here
        return picked, rank

    def reorder(picked, there):
        halves = [dot(tab[4], amps[picked[j][0] & (slots - 1)]).astype(BF16) for j in range(4)]
        for j in range(4):
            there[j] = dot(halves[j], tab[5]).astype(BF16)

    going, _ = ranked(pos, cnt[0, 0], col + 1)
    local[1].wait()
    local[3].wait()
    reorder(going, sa)
    for j in range(1):
        send(AMP + j, sa.at[j], ra.at[j], "", "right")
    home, n_home = ranked(pos, cnt[0, 0], col)
    reorder(home, held)
    corners(0, outer_half, inner_rim, "outer")

    local[2].wait()
    for k in range(modes):
        for c in range(2):
            for b in range(2):
                pp[k, c, b] = probe[pl.ds(k * 1024 + 2 * b + c, 256, stride=4), :]
    for b in range(2):
        for first in range(0, 256, 32):
            total = None
            for k in range(modes):
                for c in range(2):
                    part = pp[k, c, b, first : first + 32, :]
                    total = part * part if total is None else total + part * part
            light[b, first : first + 32, :] = total

    for c in range(2):
        pg[c, 12] = jnp.zeros((768, 128), F32)
        for n in range(12):
            for first in (0, 512):
                pg[c, n, first : first + 256, :] = jnp.zeros((256, 128), F32)
    pw[...] = jnp.zeros_like(pw)
    cw[...] = jnp.zeros_like(cw)
    for j in range(4):
        held[4 + j] = jnp.zeros((256, 256), BF16)

    for side in range(2):

        @pl.when(jnp.logical_not(has[("left", "right")[side]]))
        def _(side=side):
            for ref in (wx, gx):
                ref[:, side] = jnp.zeros(ref.shape[:1] + ref.shape[2:], BF16)

        @pl.when(jnp.logical_not(exists("outer", ("left", "right")[side])))
        def _(side=side):
            for ref in (wd, gd):
                ref[side] = jnp.zeros(ref.shape[1:], BF16)

    @pl.when(jnp.logical_not(has["outer"]))
    def _():
        for ref in (wo, go):
            ref[...] = jnp.zeros(ref.shape, BF16)

    corners(1, inner_half, outer_rim, "inner")
    for j in range(1, 4):
        send(AMP + j, sa.at[j], ra.at[j], "", "right")

    arrived(POS)
    arrived(CNT)

    @pl.when(jnp.logical_not(has["left"]))
    def _():
        left_cnt[0, 0] = 0
        for i in range(slots):
            for axis in range(2):
                left_pos[0, axis, i] = 0

    came, _ = ranked(left_pos, left_cnt[0, 0], col)
    for j in range(4):
        for i in range(2):
            table[3 + i, j] = came[j][1 + i]
    for j in range(4):
        from_left = j >= n_home
        there = jnp.clip(j - n_home, 0, 3)
        table[0, j] = jnp.where(from_left, 4 + there, j)
        for i in range(2):
            table[1 + i, j] = jnp.where(from_left, table[3 + i, there], home[j][1 + i]) & 255

    lanes = lax.broadcasted_iota(jnp.int32, (256, 128), 1)

    def spread(ref, pieces, shift):
        keep = lanes >= shift
        low, high = (pltpu.roll(piece, shift, 1) for piece in pieces)
        ref[1, 256:512, :] = jnp.where(keep, low, 0.0)
        ref[2, 256:512, :] = jnp.where(keep, high, low)
        ref[3, 256:512, :] = jnp.where(keep, 0.0, high)

    def place(canvas, ref, y, block):
        for b in range(4):
            canvas[b] += ref[b - block + 1, pl.ds(256 - y, 512), :]

    def weigh(j, carry):
        y, x = table[1, j], table[2, j]
        spread(pw, [light[0], light[1]], x & 127)
        place(cw.at[0], pw, y, x >> 7)
        return carry

    lax.fori_loop(0, 4, weigh, 0)
    widen(OBJ + 4, [1, 2], outer_rim)
    widen(OBJ + 5, [1, 2], inner_rim)
    for copy, there, block, vertical in corner_copies:
        span = outer_rim if vertical == "outer" else inner_rim

        @pl.when(there)
        def _(copy=copy, block=block, span=span):
            copy.wait_recv()
            for c in range(2):
                ext[c, block, span, :] = rim[c, block, span, :].astype(F32)

    def halo_out(base, gather, layers, stage, from_inner, from_x, from_corner, from_outer):
        def rounded(blocks, span):
            for c in range(layers):
                for b in blocks:
                    stage[c, b, span, :] = gather(c, b, span).astype(BF16)

        rounded(range(4), inner_rim)
        send(base, stage.at[:, :, inner_rim], from_inner, "inner", "")
        rounded((0, 3), outer_half)
        for n, (side, block) in enumerate((("right", 3), ("left", 0))):
            send(base + 1 + n, stage.at[:, block, outer_half], from_x.at[0, n], "", side)
        rounded(range(4), outer_rim)
        for n, (side, block) in enumerate((("right", 3), ("left", 0))):
            send(base + 3 + n, stage.at[:, block, outer_rim], from_corner.at[n], "outer", side)
        send(base + 5, stage.at[:, pl.ds(1, 2), outer_rim], from_outer, "outer", "")

    def halo_inner(base, gather, layers, stage, from_inner, from_x):
        arrived(base)
        for n, (side, block) in enumerate((("right", 3), ("left", 0))):
            for c in range(layers):
                total = gather(c, block, inner_half) + from_inner[c, block].astype(F32)
                stage[c, block, inner_half, :] = total.astype(BF16)
            send(base + 6 + n, stage.at[:, block, inner_half], from_x.at[1, n], "", side)

    def weight_at(c, b, span):
        return cw[c, b, span, :]

    halo_out(WEIGHT, weight_at, 1, ws, wi, wx, wd, wo)

    def cut_window(j):
        y, x = table[1, j], table[2, j]
        block, shift = x >> 7, x & 127
        keep = lax.broadcasted_iota(jnp.int32, (64, 128), 1) >= shift
        for c in range(2):
            for b in range(2):
                for first in range(0, 256, 64):
                    near = ext[c, block + b, pl.ds(y + first, 64), :]
                    beyond = ext[c, block + b + 1, pl.ds(y + first, 64), :]
                    win[c, b, first : first + 64, :] = pltpu.roll(
                        jnp.where(keep, near, beyond), (128 - shift) & 127, 1
                    )


    def exit_waves():
        def piece(first, k):
            cut = slice(first, first + 16)
            at = 2 * first if first < 128 else 2 * (first - 128) + 16
            waves = []
            for b in range(2):
                p_re, p_im, w_re, w_im = pp[k, 0, b, cut, :], pp[k, 1, b, cut, :], win[0, b, cut, :], win[1, b, cut, :]
                waves.append((p_re * w_re - p_im * w_im, p_re * w_im + p_im * w_re))
            to_rows = slice(256 * k + at, 256 * k + at + 16)
            for part in range(2):
                low, high = waves[0][part], waves[1][part]
                lanes_of = slice(128 * part, 128 * part + 128)
                wave[0, to_rows, lanes_of] = (low + high).astype(BF16)
                wave[1, to_rows, lanes_of] = (low - high).astype(BF16)

        return [functools.partial(piece, first, k) for first in range(0, 256, 16) for k in range(modes)]

    def half_done():
        done = {}

        def product(parity):
            done[parity] = dot(wave[parity], tab[parity])

        def piece(parity, k, first):
            lanes_of = slice(128 * parity, 128 * parity + 128)
            at = 256 * k + 2 * first
            low, high = done[parity][at : at + 16], done[parity][at + 16 : at + 32]
            plus, minus = (low + high).astype(BF16), (low - high).astype(BF16)
            for part in range(2):
                to_rows = slice(128 * part + first, 128 * part + first + 16)
                source = slice(128 * part, 128 * part + 128)
                stack[0, k, to_rows, lanes_of] = plus[:, source]
                stack[1, k, to_rows, lanes_of] = minus[:, source]

        pieces = []
        for parity in range(2):
            pieces.append(functools.partial(product, parity))
            pieces += [functools.partial(piece, parity, k, f) for k in range(modes) for f in range(0, 128, 16)]
        return pieces

    def far_field():
        def piece(parity, k):
            far[parity, k] = dot(tab[2 + parity], stack[parity, k])

        return [functools.partial(piece, parity, k) for parity in range(2) for k in range(modes)]

    def residue(parity, amplitude):
        for first in range(0, 128, 16):
            upper, lower = slice(first, first + 16), slice(128 + first, 144 + first)
            re = [far[parity, k, upper, :] for k in range(modes)]
            im = [far[parity, k, lower, :] for k in range(modes)]
            intensity = None
            for k in range(modes):
                term = re[k] * re[k] + im[k] * im[k]
                intensity = term if intensity is None else intensity + term
            held = lax.rsqrt(jnp.maximum(intensity, floor_amplitude * floor_amplitude))
            measured = amplitude[128 * parity + first : 128 * parity + first + 16, :].astype(F32)
            factor = 1.0 - measured * held
            for k in range(modes):
                turned[parity, k, upper, :] = (re[k] * factor).astype(BF16)
                turned[parity, k, lower, :] = (im[k] * factor).astype(BF16)

    def near_field():
        done = {}

        def product(parity, k):
            done[parity, k] = dot(tab[parity], turned[parity, k])

        def piece(k, first):
            cut = slice(first, first + 16)
            part, at = first // 128, 256 * k + first % 128
            lanes_of = slice(128 * part, 128 * part + 128)
            even, odd = done[0, k][cut], done[1, k][cut]
            plus, minus = (even + odd).astype(BF16), (even - odd).astype(BF16)
            for column in range(2):
                source = slice(128 * column, 128 * column + 128)
                near[column, at : at + 16, lanes_of] = plus[:, source]
                near[column, 128 + at : 144 + at, lanes_of] = minus[:, source]

        pieces = []
        for k in range(modes):
            pieces += [functools.partial(product, parity, k) for parity in range(2)]
            pieces += [functools.partial(piece, k, first) for first in range(0, 256, 16)]
        return pieces

    def back_parts():
        def piece(parity):
            back = dot(near[parity], tab[2 + parity])
            for k in range(modes):
                ends[parity, k] = back[256 * k : 256 * k + 256]

        return [functools.partial(piece, parity) for parity in range(2)]

    def gradient():
        def piece(first):
            cut = slice(first, first + 16)
            total = [None] * 4
            for k in range(modes):
                e_re, o_re = ends[0, k, cut, 0:128], ends[1, k, cut, 0:128]
                e_im, o_im = ends[0, k, cut, 128:256], ends[1, k, cut, 128:256]
                for b in range(2):
                    b_re = e_re + o_re if b == 0 else e_re - o_re
                    b_im = e_im + o_im if b == 0 else e_im - o_im
                    p_re, p_im = pp[k, 0, b, cut, :], pp[k, 1, b, cut, :]
                    for n, term in ((b, p_re * b_re + p_im * b_im), (2 + b, p_re * b_im - p_im * b_re)):
                        total[n] = term if total[n] is None else total[n] + term
            for b in range(2):
                grad[0, b, cut, :] = total[b]
                grad[1, b, cut, :] = total[2 + b]

        return [functools.partial(piece, first) for first in range(0, 256, 16)]

    def take_turns(*stages):
        marked = [((n + 0.5) / len(stage), m, piece) for m, stage in enumerate(stages) for n, piece in enumerate(stage)]
        for _, _, piece in sorted(marked, key=lambda entry: entry[:2]):
            piece()

    def keep_gradient(j):
        shift = table[2, j] & 127
        for first in range(0, 256, 64):
            cut, at = slice(first, first + 64), slice(256 + first, 320 + first)
            keep = lax.broadcasted_iota(jnp.int32, (64, 128), 1) >= shift
            for c in range(2):
                low, high = (pltpu.roll(grad[c, b, cut, :], shift, 1) for b in range(2))
                pg[c, 3 * j, at, :] = jnp.where(keep, low, 0.0)
                pg[c, 3 * j + 1, at, :] = jnp.where(keep, high, low)
                pg[c, 3 * j + 2, at, :] = jnp.where(keep, 0.0, high)

    def start_window(j):
        cut_window(j)
        take_turns(exit_waves())
        take_turns(half_done())
        take_turns(far_field())

    def factor_window(j):
        @pl.when(has["left"])
        def _():
            remote(AMP + j, sa.at[j], ra.at[j], "", "right").wait_recv()
            held[4 + j] = ra[j]

        amplitude = held.at[table[0, j]]
        for parity in range(2):
            residue(parity, amplitude)

    def slot(j, carry):
        factor_window(j)
        cut_window(j + 1)
        take_turns(near_field(), exit_waves())
        take_turns(half_done())
        take_turns(back_parts())
        take_turns(far_field(), gradient())
        keep_gradient(j)
        return carry

    start_window(0)
    lax.fori_loop(0, 3, slot, 0)
    halo_inner(WEIGHT, weight_at, 1, ws, wi, wx)
    factor_window(3)
    for stage in (near_field, back_parts, gradient):
        take_turns(stage())
    keep_gradient(3)

    def gradient_at(c, b, span):
        total = None
        for j in range(4):
            y, block = table[1, j], table[2, j] >> 7
            inside = (b >= block) & (b < block + 3)
            part = pg[c, jnp.where(inside, 3 * j + b - block, 12), pl.ds(256 - y + span.start, 128), :]
            total = part if total is None else total + part
        return total

    halo_out(GRAD, gradient_at, 2, gs, gi, gx, gd, go)
    halo_inner(GRAD, gradient_at, 2, gs, gi, gx)

    def whole(gather, c, b, from_inner, from_x, from_corner, from_outer):
        total = gather(c, 1 + b, outer_half) + from_outer[c, b].astype(F32)
        total = total + from_x[0, b, c].astype(F32) + from_corner[b, c].astype(F32)
        other = gather(c, 1 + b, inner_half) + from_inner[c, 1 + b].astype(F32)
        return total, other + from_x[1, b, c].astype(F32)

    for c in range(2):
        for b in (1, 2):
            for span in (outer_half, inner_half):
                cv[c, b, span, :] = gradient_at(c, b, span)

    def own_gradient(c, b, span):
        return cv[c, b, span, :]

    for number in range(1, 8):
        arrived(WEIGHT + number)
    for b in range(2):
        far_half, near_half = whole(weight_at, 0, b, wi, wx, wd, wo)
        cw[0, 1 + b, outer_half, :] = 1.0 / (far_half + ridge_weight)
        cw[0, 1 + b, inner_half, :] = 1.0 / (near_half + ridge_weight)
    for number in range(1, 8):
        arrived(GRAD + number)
    for c in range(2):
        for b in range(2):
            far_half, near_half = whole(own_gradient, c, b, gi, gx, gd, go)
            first, second = 512 * core + 2 * b + c, 512 - 512 * core + 2 * b + c
            out[pl.ds(first, 128, stride=4), :] = far_half * cw[0, 1 + b, outer_half, :]
            out[pl.ds(second, 128, stride=4), :] = near_half * cw[0, 1 + b, inner_half, :]

    for copy, vertical, across in sent.values():
        pl.when(exists(vertical, across))(copy.wait_send)
    for copy, there, _, _ in corner_copies:
        pl.when(there)(copy.wait_send)


def on_device(n_row, n_col, object_field, probe_modes, amplitudes, positions, counts):
    modes, extent = probe_modes.shape[0], probe_modes.shape[1]
    slots = amplitudes.shape[1]
    half = extent // 2
    obj = object_field.reshape(extent, 2, 2, half).transpose(0, 2, 1, 3).reshape(4 * extent, half)
    probe = probe_modes.reshape(modes, extent, 2, 2, half).transpose(0, 1, 3, 2, 4)
    probe = probe.reshape(modes * 4 * extent, half)
    tab = jnp.asarray(tables(extent))
    big = 2 * extent
    vmem, anywhere = pltpu.VMEM, pl.BlockSpec(memory_space=pl.ANY)
    scratch = [
        pltpu.SMEM((1, 2, slots), jnp.int32),
        pltpu.SMEM((1, 1), jnp.int32),
        vmem((4 * extent, half), F32),
        vmem((modes * 4 * extent, half), F32),
        vmem((slots, extent, extent), BF16),
        vmem((8, extent, extent), BF16),
        vmem((6, extent, extent), BF16),
        vmem((modes, 2, 2, extent, half), F32),
        vmem((2, extent, half), F32),
        vmem((2, 4, big, half), F32),
        vmem((2, 2, extent, half), F32),
        vmem((2, 4, big, half), BF16),
        vmem((4, extent, extent), BF16),
        vmem((4, extent, extent), BF16),
        pltpu.SMEM((1, 2, slots), jnp.int32),
        pltpu.SMEM((1, 1), jnp.int32),
        pltpu.SMEM((5, 4), jnp.int32),
        vmem((2, modes, extent, extent), F32),
        vmem((2, modes, extent, extent), F32),
        vmem((2, modes * extent, extent), BF16),
        vmem((2, modes * extent, extent), BF16),
        vmem((2, modes, extent, extent), BF16),
        vmem((2, modes, extent, extent), BF16),
        vmem((2, 2, extent, half), F32),
        vmem((2, 13, 3 * extent, half), F32),
        vmem((5, 3 * extent, half), F32),
        vmem((2, 4, big, half), F32),
        vmem((1, 4, big, half), F32),
        vmem((1, 4, big, half), BF16),
        vmem((1, 4, half, half), BF16),
        vmem((2, 2, 1, half, half), BF16),
        vmem((2, 1, half, half), BF16),
        vmem((1, 2, half, half), BF16),
        vmem((2, 4, big, half), BF16),
        vmem((2, 4, half, half), BF16),
        vmem((2, 2, 2, half, half), BF16),
        vmem((2, 2, half, half), BF16),
        vmem((2, 2, half, half), BF16),
        pltpu.SemaphoreType.DMA((6,)),
        pltpu.SemaphoreType.DMA((COPIES,)),
        pltpu.SemaphoreType.DMA((COPIES,)),
    ]
    update = pl.pallas_call(
        functools.partial(kernel, n_row, n_col, slots, modes),
        out_shape=pltpu.VMEM((4 * extent, half), F32),
        in_specs=[anywhere] * 6,
        out_specs=pl.BlockSpec(memory_space=pltpu.VMEM),
        scratch_shapes=scratch,
        compiler_params=pltpu.CompilerParams(
            collective_id=0, has_side_effects=True, vmem_limit_bytes=56 * 1024 * 1024
        ),
        cost_estimate=pl.CostEstimate(flops=5 * 10**9, bytes_accessed=5 * 10**6, transcendentals=3 * 10**5),
    )(obj, probe, amplitudes[0], tab, positions.transpose(0, 2, 1), counts)
    return update.reshape(extent, 2, 2, half).transpose(0, 2, 1, 3).reshape(extent, 2, extent)


def solution(mesh):
    in_specs = (
        P("row", None, "col"),
        P(),
        P("row", "col", None, None),
        P("row", "col", None),
        P("row", "col"),
    )
    out_specs = P("row", None, "col")
    step = functools.partial(on_device, mesh.shape["row"], mesh.shape["col"])
    return jax.shard_map(step, mesh=mesh, in_specs=in_specs, out_specs=out_specs, check_vma=False)
```

```python
import functools

import jax
import jax.numpy as jnp
import numpy as np
from jax import lax
from jax.experimental import pallas as pl
from jax.experimental.pallas import tpu as pltpu
from jax.sharding import PartitionSpec as P

MESH = pl.DeviceIdType.MESH
F32 = jnp.float32
BF16 = jnp.bfloat16

floor_amplitude = 0.25
ridge_weight = 1.0

POS, CNT = 0, 1
OBJ = 2
CORNER = 8
AMP = 12
WEIGHT = 16
GRAD = 24
COPIES = 32
RIGHT, LEFT = (0, 1), (0, -1)


def tables(extent):
    half = extent // 2
    steps = np.arange(extent)
    turns = np.outer(np.arange(half), steps) % extent
    scale = 1.0 / np.sqrt(extent)
    cosine = np.cos(2.0 * np.pi * turns / extent) * scale
    sine = np.sin(2.0 * np.pi * turns / extent) * scale
    forward = []
    for parity in range(2):
        c, s = cosine[:, parity::2], sine[:, parity::2]
        forward.append(np.block([[c, -s], [s, c]]))
    order = np.concatenate([steps[0::2], steps[1::2]])
    permute = np.eye(extent)[order]
    stack = [forward[0], forward[1], forward[0].T, forward[1].T, permute, permute.T]
    return np.stack(stack).astype(np.float32).astype(jnp.bfloat16)


def dot(a, b):
    return jnp.dot(a, b, preferred_element_type=F32)


def kernel(
    n_row, n_col, slots, modes,
    obj_hbm, probe_hbm, amp_hbm, tab_hbm, pos_hbm, cnt_hbm, out,
    pos, cnt, obj, probe, amps, held, tab, pp, light, ext, win,
    rim, sa, ra, left_pos, left_cnt, table,
    far, ends, wave, near, stack, turned, grad, pg, pw, cv, cw,
    ws, wi, wx, wd, wo, gs, gi, gx, gd, go,
    lsem, ssem, rsem,
):
    row, col = lax.axis_index("row"), lax.axis_index("col")
    core = lax.rem(row, 2)
    outer, inner = 2 * core - 1, 1 - 2 * core
    has = {
        "right": col < n_col - 1, "left": col > 0,
        "outer": jnp.where(core == 0, row > 0, row < n_row - 1), "inner": row >= 0,
    }
    sides = (("right", 1), ("left", -1))

    def to(vertical, across):
        step = {"outer": outer, "inner": inner, "": 0}[vertical]
        return (row + step, col + {"right": 1, "left": -1, "": 0}[across])

    def exists(vertical, across):
        if vertical and across:
            return has[vertical] & has[across]
        return has[vertical or across]

    def opposite(across):
        return {"right": "left", "left": "right", "": ""}[across]

    def remote(number, src, dst, vertical, across):
        return pltpu.make_async_remote_copy(
            src_ref=src, dst_ref=dst, send_sem=ssem.at[number], recv_sem=rsem.at[number],
            device_id=to(vertical, across), device_id_type=MESH,
        )

    sent = {}

    def send(number, src, dst, vertical, across):
        copy = remote(number, src, dst, vertical, across)
        pl.when(exists(vertical, across))(copy.start)
        sent[number] = (copy, vertical, across)

    def arrived(number):
        copy, vertical, across = sent[number]
        pl.when(exists(vertical, opposite(across)))(copy.wait_recv)

    def rows(start):
        return pl.ds(pl.multiple_of(start, 128), 128)

    outer_half, inner_half = rows(128 + 128 * core), rows(256 - 128 * core)
    outer_rim, inner_rim = rows(384 * core), rows(384 - 384 * core)

    local = [
        pltpu.make_async_copy(obj_hbm, obj, lsem.at[0]),
        pltpu.make_async_copy(amp_hbm, amps, lsem.at[1]),
        pltpu.make_async_copy(probe_hbm, probe, lsem.at[2]),
        pltpu.make_async_copy(tab_hbm, tab, lsem.at[3]),
        pltpu.make_async_copy(pos_hbm, pos, lsem.at[4]),
        pltpu.make_async_copy(cnt_hbm, cnt, lsem.at[5]),
    ]
    for n in (0, 4, 5):
        local[n].start()

    barrier = pltpu.get_barrier_semaphore()
    for vertical, across in (("", "right"), ("", "left"), ("outer", ""), ("inner", "")):
        pl.when(exists(vertical, across))(
            functools.partial(
                pl.semaphore_signal, barrier, inc=1, device_id=to(vertical, across), device_id_type=MESH
            )
        )

    for c in range(2):
        for b in (0, 3):
            ext[c, b] = jnp.zeros((512, 128), F32)
        for b in (1, 2):
            ext[c, b, 0:128, :] = jnp.zeros((128, 128), F32)
            ext[c, b, 384:512, :] = jnp.zeros((128, 128), F32)
    local[0].wait()
    for n in (1, 3, 2):
        local[n].start()
    for c in range(2):
        for b in range(2):
            plane = obj[pl.ds(2 * b + c, 256, stride=4), :]
            ext[c, 1 + b, 128:384, :] = plane
            rim[c, 1 + b, 128:384, :] = plane.astype(BF16)

    neighbours = jnp.int32(1)
    for name in ("right", "left", "outer"):
        neighbours = neighbours + jnp.where(has[name], 1, 0)
    pl.semaphore_wait(barrier, neighbours)

    local[4].wait()
    local[5].wait()
    send(POS, pos, left_pos, "", "right")
    send(CNT, cnt, left_cnt, "", "right")
    for n, half in enumerate((outer_half, inner_half)):
        send(OBJ + 2 * n, rim.at[:, 2, half], rim.at[:, 0, half], "", "right")
        send(OBJ + 2 * n + 1, rim.at[:, 1, half], rim.at[:, 3, half], "", "left")
    send(OBJ + 4, rim.at[:, pl.ds(1, 2), outer_half], rim.at[:, pl.ds(1, 2), inner_rim], "outer", "")
    send(OBJ + 5, rim.at[:, pl.ds(1, 2), inner_half], rim.at[:, pl.ds(1, 2), outer_rim], "inner", "")

    def widen(number, blocks, span):
        copy, vertical, across = sent[number]

        @pl.when(exists(vertical, opposite(across)))
        def _():
            copy.wait_recv()
            for c in range(2):
                for b in blocks:
                    ext[c, b, span, :] = rim[c, b, span, :].astype(F32)

    def corners(n, half, beyond, vertical):
        for m, (side, block) in enumerate((("left", 0), ("right", 3))):
            widen(OBJ + 2 * n + m, [block], half)
            copy = remote(CORNER + 2 * n + m, rim.at[:, block, half], rim.at[:, block, beyond], vertical, "")
            there = exists(vertical, side)
            pl.when(there)(copy.start)
            corner_copies.append((copy, there, block, vertical))

    corner_copies = []

    def ranked(ref, count, tile):
        rank = jnp.int32(0)
        picked = [[jnp.int32(0)] * 3 for _ in range(4)]
        for i in range(slots):
            y, x = ref[0, 0, i], ref[0, 1, i]
            here = jnp.where((i < count) & ((x >> 8) == tile), 1, 0)
            for j in range(4):
                hit = jnp.where(rank == j, here, 0)
                picked[j] = [old + hit * new for old, new in zip(picked[j], (i, y, x))]
            rank = rank + here
        return picked, rank

    def reorder(picked, there):
        halves = [dot(tab[4], amps[picked[j][0] & (slots - 1)]).astype(BF16) for j in range(4)]
        for j in range(4):
            there[j] = dot(halves[j], tab[5]).astype(BF16)

    going, _ = ranked(pos, cnt[0, 0], col + 1)
    local[1].wait()
    local[3].wait()
    reorder(going, sa)
    for j in range(1):
        send(AMP + j, sa.at[j], ra.at[j], "", "right")
    home, n_home = ranked(pos, cnt[0, 0], col)
    reorder(home, held)
    corners(0, outer_half, inner_rim, "outer")

    local[2].wait()
    for k in range(modes):
        for c in range(2):
            for b in range(2):
                pp[k, c, b] = probe[pl.ds(k * 1024 + 2 * b + c, 256, stride=4), :]
    for b in range(2):
        for first in range(0, 256, 32):
            total = None
            for k in range(modes):
                for c in range(2):
                    part = pp[k, c, b, first : first + 32, :]
                    total = part * part if total is None else total + part * part
            light[b, first : first + 32, :] = total

    for c in range(2):
        pg[c, 12] = jnp.zeros((768, 128), F32)
        for n in range(12):
            for first in (0, 512):
                pg[c, n, first : first + 256, :] = jnp.zeros((256, 128), F32)
    pw[...] = jnp.zeros_like(pw)
    cw[...] = jnp.zeros_like(cw)
    for j in range(4):
        held[4 + j] = jnp.zeros((256, 256), BF16)

    for side in range(2):

        @pl.when(jnp.logical_not(has[("left", "right")[side]]))
        def _(side=side):
            for ref in (wx, gx):
                ref[:, side] = jnp.zeros(ref.shape[:1] + ref.shape[2:], BF16)

        @pl.when(jnp.logical_not(exists("outer", ("left", "right")[side])))
        def _(side=side):
            for ref in (wd, gd):
                ref[side] = jnp.zeros(ref.shape[1:], BF16)

    @pl.when(jnp.logical_not(has["outer"]))
    def _():
        for ref in (wo, go):
            ref[...] = jnp.zeros(ref.shape, BF16)

    corners(1, inner_half, outer_rim, "inner")
    for j in range(1, 4):
        send(AMP + j, sa.at[j], ra.at[j], "", "right")

    arrived(POS)
    arrived(CNT)

    @pl.when(jnp.logical_not(has["left"]))
    def _():
        left_cnt[0, 0] = 0
        for i in range(slots):
            for axis in range(2):
                left_pos[0, axis, i] = 0

    came, _ = ranked(left_pos, left_cnt[0, 0], col)
    for j in range(4):
        for i in range(2):
            table[3 + i, j] = came[j][1 + i]
    for j in range(4):
        from_left = j >= n_home
        there = jnp.clip(j - n_home, 0, 3)
        table[0, j] = jnp.where(from_left, 4 + there, j)
        for i in range(2):
            table[1 + i, j] = jnp.where(from_left, table[3 + i, there], home[j][1 + i]) & 255

    lanes = lax.broadcasted_iota(jnp.int32, (256, 128), 1)

    def spread(ref, pieces, shift):
        keep = lanes >= shift
        low, high = (pltpu.roll(piece, shift, 1) for piece in pieces)
        ref[1, 256:512, :] = jnp.where(keep, low, 0.0)
        ref[2, 256:512, :] = jnp.where(keep, high, low)
        ref[3, 256:512, :] = jnp.where(keep, 0.0, high)

    def place(canvas, ref, y, block):
        for b in range(4):
            canvas[b] += ref[b - block + 1, pl.ds(256 - y, 512), :]

    def weigh(j, carry):
        y, x = table[1, j], table[2, j]
        spread(pw, [light[0], light[1]], x & 127)
        place(cw.at[0], pw, y, x >> 7)
        return carry

    lax.fori_loop(0, 4, weigh, 0)
    widen(OBJ + 4, [1, 2], outer_rim)
    widen(OBJ + 5, [1, 2], inner_rim)
    for copy, there, block, vertical in corner_copies:
        span = outer_rim if vertical == "outer" else inner_rim

        @pl.when(there)
        def _(copy=copy, block=block, span=span):
            copy.wait_recv()
            for c in range(2):
                ext[c, block, span, :] = rim[c, block, span, :].astype(F32)

    def halo_out(base, gather, layers, stage, from_inner, from_x, from_corner, from_outer):
        def rounded(blocks, span):
            for c in range(layers):
                for b in blocks:
                    stage[c, b, span, :] = gather(c, b, span).astype(BF16)

        rounded(range(4), inner_rim)
        send(base, stage.at[:, :, inner_rim], from_inner, "inner", "")
        rounded((0, 3), outer_half)
        for n, (side, block) in enumerate((("right", 3), ("left", 0))):
            send(base + 1 + n, stage.at[:, block, outer_half], from_x.at[0, n], "", side)
        rounded(range(4), outer_rim)
        for n, (side, block) in enumerate((("right", 3), ("left", 0))):
            send(base + 3 + n, stage.at[:, block, outer_rim], from_corner.at[n], "outer", side)
        send(base + 5, stage.at[:, pl.ds(1, 2), outer_rim], from_outer, "outer", "")

    def halo_inner(base, gather, layers, stage, from_inner, from_x):
        arrived(base)
        for n, (side, block) in enumerate((("right", 3), ("left", 0))):
            for c in range(layers):
                total = gather(c, block, inner_half) + from_inner[c, block].astype(F32)
                stage[c, block, inner_half, :] = total.astype(BF16)
            send(base + 6 + n, stage.at[:, block, inner_half], from_x.at[1, n], "", side)

    def weight_at(c, b, span):
        return cw[c, b, span, :]

    halo_out(WEIGHT, weight_at, 1, ws, wi, wx, wd, wo)

    def cut_window(j):
        y, x = table[1, j], table[2, j]
        block, shift = x >> 7, x & 127
        keep = lax.broadcasted_iota(jnp.int32, (64, 128), 1) >= shift
        for c in range(2):
            for b in range(2):
                for first in range(0, 256, 64):
                    near = ext[c, block + b, pl.ds(y + first, 64), :]
                    beyond = ext[c, block + b + 1, pl.ds(y + first, 64), :]
                    win[c, b, first : first + 64, :] = pltpu.roll(
                        jnp.where(keep, near, beyond), (128 - shift) & 127, 1
                    )


    def exit_waves():
        def piece(first):
            cut = slice(first, first + 16)
            at = 2 * first if first < 128 else 2 * (first - 128) + 16
            w_re, w_im = [win[0, b, cut, :] for b in range(2)], [win[1, b, cut, :] for b in range(2)]
            for k in range(modes):
                waves = []
                for b in range(2):
                    p_re, p_im = pp[k, 0, b, cut, :], pp[k, 1, b, cut, :]
                    waves.append((p_re * w_re[b] - p_im * w_im[b], p_re * w_im[b] + p_im * w_re[b]))
                to_rows = slice(256 * k + at, 256 * k + at + 16)
                for part in range(2):
                    low, high = waves[0][part], waves[1][part]
                    lanes_of = slice(128 * part, 128 * part + 128)
                    wave[0, to_rows, lanes_of] = (low + high).astype(BF16)
                    wave[1, to_rows, lanes_of] = (low - high).astype(BF16)

        return [functools.partial(piece, first) for first in range(0, 256, 16)]

    def half_done():
        done = {}

        def product(parity):
            done[parity] = dot(wave[parity], tab[parity])

        def piece(parity, k, first):
            lanes_of = slice(128 * parity, 128 * parity + 128)
            at = 256 * k + 2 * first
            low, high = done[parity][at : at + 16], done[parity][at + 16 : at + 32]
            plus, minus = (low + high).astype(BF16), (low - high).astype(BF16)
            for part in range(2):
                to_rows = slice(128 * part + first, 128 * part + first + 16)
                source = slice(128 * part, 128 * part + 128)
                stack[0, k, to_rows, lanes_of] = plus[:, source]
                stack[1, k, to_rows, lanes_of] = minus[:, source]

        pieces = []
        for parity in range(2):
            pieces.append(functools.partial(product, parity))
            pieces += [functools.partial(piece, parity, k, f) for k in range(modes) for f in range(0, 128, 16)]
        return pieces

    def far_field():
        def piece(parity, k):
            far[parity, k] = dot(tab[2 + parity], stack[parity, k])

        return [functools.partial(piece, parity, k) for parity in range(2) for k in range(modes)]

    def residue(parity, amplitude):
        for first in range(0, 128, 16):
            upper, lower = slice(first, first + 16), slice(128 + first, 144 + first)
            re = [far[parity, k, upper, :] for k in range(modes)]
            im = [far[parity, k, lower, :] for k in range(modes)]
            intensity = None
            for k in range(modes):
                term = re[k] * re[k] + im[k] * im[k]
                intensity = term if intensity is None else intensity + term
            held = lax.rsqrt(jnp.maximum(intensity, floor_amplitude * floor_amplitude))
            measured = amplitude[128 * parity + first : 128 * parity + first + 16, :].astype(F32)
            factor = 1.0 - measured * held
            for k in range(modes):
                turned[parity, k, upper, :] = (re[k] * factor).astype(BF16)
                turned[parity, k, lower, :] = (im[k] * factor).astype(BF16)

    def near_field():
        done = {}

        def product(parity, k):
            done[parity, k] = dot(tab[parity], turned[parity, k])

        def piece(k, first):
            cut = slice(first, first + 16)
            part, at = first // 128, 256 * k + first % 128
            lanes_of = slice(128 * part, 128 * part + 128)
            even, odd = done[0, k][cut], done[1, k][cut]
            plus, minus = (even + odd).astype(BF16), (even - odd).astype(BF16)
            for column in range(2):
                source = slice(128 * column, 128 * column + 128)
                near[column, at : at + 16, lanes_of] = plus[:, source]
                near[column, 128 + at : 144 + at, lanes_of] = minus[:, source]

        pieces = []
        for k in range(modes):
            pieces += [functools.partial(product, parity, k) for parity in range(2)]
            pieces += [functools.partial(piece, k, first) for first in range(0, 256, 16)]
        return pieces

    def back_parts():
        def piece(parity):
            back = dot(near[parity], tab[2 + parity])
            for k in range(modes):
                ends[parity, k] = back[256 * k : 256 * k + 256]

        return [functools.partial(piece, parity) for parity in range(2)]

    def gradient():
        def piece(first):
            cut = slice(first, first + 16)
            total = [None] * 4
            for k in range(modes):
                e_re, o_re = ends[0, k, cut, 0:128], ends[1, k, cut, 0:128]
                e_im, o_im = ends[0, k, cut, 128:256], ends[1, k, cut, 128:256]
                for b in range(2):
                    b_re = e_re + o_re if b == 0 else e_re - o_re
                    b_im = e_im + o_im if b == 0 else e_im - o_im
                    p_re, p_im = pp[k, 0, b, cut, :], pp[k, 1, b, cut, :]
                    for n, term in ((b, p_re * b_re + p_im * b_im), (2 + b, p_re * b_im - p_im * b_re)):
                        total[n] = term if total[n] is None else total[n] + term
            for b in range(2):
                grad[0, b, cut, :] = total[b]
                grad[1, b, cut, :] = total[2 + b]

        return [functools.partial(piece, first) for first in range(0, 256, 16)]

    def take_turns(*stages):
        marked = [((n + 0.5) / len(stage), m, piece) for m, stage in enumerate(stages) for n, piece in enumerate(stage)]
        for _, _, piece in sorted(marked, key=lambda entry: entry[:2]):
            piece()

    def keep_gradient(j):
        shift = table[2, j] & 127
        for first in range(0, 256, 64):
            cut, at = slice(first, first + 64), slice(256 + first, 320 + first)
            keep = lax.broadcasted_iota(jnp.int32, (64, 128), 1) >= shift
            for c in range(2):
                low, high = (pltpu.roll(grad[c, b, cut, :], shift, 1) for b in range(2))
                pg[c, 3 * j, at, :] = jnp.where(keep, low, 0.0)
                pg[c, 3 * j + 1, at, :] = jnp.where(keep, high, low)
                pg[c, 3 * j + 2, at, :] = jnp.where(keep, 0.0, high)

    def start_window(j):
        cut_window(j)
        take_turns(exit_waves())
        take_turns(half_done())
        take_turns(far_field())

    def factor_window(j):
        @pl.when(has["left"])
        def _():
            remote(AMP + j, sa.at[j], ra.at[j], "", "right").wait_recv()
            held[4 + j] = ra[j]

        amplitude = held.at[table[0, j]]
        for parity in range(2):
            residue(parity, amplitude)

    def slot(j, carry):
        factor_window(j)
        cut_window(j + 1)
        take_turns(near_field(), exit_waves())
        take_turns(half_done())
        take_turns(back_parts())
        take_turns(far_field(), gradient())
        keep_gradient(j)
        return carry

    start_window(0)
    lax.fori_loop(0, 3, slot, 0)
    halo_inner(WEIGHT, weight_at, 1, ws, wi, wx)
    factor_window(3)
    for stage in (near_field, back_parts, gradient):
        take_turns(stage())
    keep_gradient(3)

    def gradient_at(c, b, span):
        total = None
        for j in range(4):
            y, block = table[1, j], table[2, j] >> 7
            inside = (b >= block) & (b < block + 3)
            part = pg[c, jnp.where(inside, 3 * j + b - block, 12), pl.ds(256 - y + span.start, 128), :]
            total = part if total is None else total + part
        return total

    halo_out(GRAD, gradient_at, 2, gs, gi, gx, gd, go)
    halo_inner(GRAD, gradient_at, 2, gs, gi, gx)

    def whole(gather, c, b, from_inner, from_x, from_corner, from_outer):
        total = gather(c, 1 + b, outer_half) + from_outer[c, b].astype(F32)
        total = total + from_x[0, b, c].astype(F32) + from_corner[b, c].astype(F32)
        other = gather(c, 1 + b, inner_half) + from_inner[c, 1 + b].astype(F32)
        return total, other + from_x[1, b, c].astype(F32)

    for c in range(2):
        for b in (1, 2):
            for span in (outer_half, inner_half):
                cv[c, b, span, :] = gradient_at(c, b, span)

    def own_gradient(c, b, span):
        return cv[c, b, span, :]

    for number in range(1, 8):
        arrived(WEIGHT + number)
    for b in range(2):
        far_half, near_half = whole(weight_at, 0, b, wi, wx, wd, wo)
        cw[0, 1 + b, outer_half, :] = 1.0 / (far_half + ridge_weight)
        cw[0, 1 + b, inner_half, :] = 1.0 / (near_half + ridge_weight)
    for number in range(1, 8):
        arrived(GRAD + number)
    for c in range(2):
        for b in range(2):
            far_half, near_half = whole(own_gradient, c, b, gi, gx, gd, go)
            first, second = 512 * core + 2 * b + c, 512 - 512 * core + 2 * b + c
            out[pl.ds(first, 128, stride=4), :] = far_half * cw[0, 1 + b, outer_half, :]
            out[pl.ds(second, 128, stride=4), :] = near_half * cw[0, 1 + b, inner_half, :]

    for copy, vertical, across in sent.values():
        pl.when(exists(vertical, across))(copy.wait_send)
    for copy, there, _, _ in corner_copies:
        pl.when(there)(copy.wait_send)


def on_device(n_row, n_col, object_field, probe_modes, amplitudes, positions, counts):
    modes, extent = probe_modes.shape[0], probe_modes.shape[1]
    slots = amplitudes.shape[1]
    half = extent // 2
    obj = object_field.reshape(extent, 2, 2, half).transpose(0, 2, 1, 3).reshape(4 * extent, half)
    probe = probe_modes.reshape(modes, extent, 2, 2, half).transpose(0, 1, 3, 2, 4)
    probe = probe.reshape(modes * 4 * extent, half)
    tab = jnp.asarray(tables(extent))
    big = 2 * extent
    vmem, anywhere = pltpu.VMEM, pl.BlockSpec(memory_space=pl.ANY)
    scratch = [
        pltpu.SMEM((1, 2, slots), jnp.int32),
        pltpu.SMEM((1, 1), jnp.int32),
        vmem((4 * extent, half), F32),
        vmem((modes * 4 * extent, half), F32),
        vmem((slots, extent, extent), BF16),
        vmem((8, extent, extent), BF16),
        vmem((6, extent, extent), BF16),
        vmem((modes, 2, 2, extent, half), F32),
        vmem((2, extent, half), F32),
        vmem((2, 4, big, half), F32),
        vmem((2, 2, extent, half), F32),
        vmem((2, 4, big, half), BF16),
        vmem((4, extent, extent), BF16),
        vmem((4, extent, extent), BF16),
        pltpu.SMEM((1, 2, slots), jnp.int32),
        pltpu.SMEM((1, 1), jnp.int32),
        pltpu.SMEM((5, 4), jnp.int32),
        vmem((2, modes, extent, extent), F32),
        vmem((2, modes, extent, extent), F32),
        vmem((2, modes * extent, extent), BF16),
        vmem((2, modes * extent, extent), BF16),
        vmem((2, modes, extent, extent), BF16),
        vmem((2, modes, extent, extent), BF16),
        vmem((2, 2, extent, half), F32),
        vmem((2, 13, 3 * extent, half), F32),
        vmem((5, 3 * extent, half), F32),
        vmem((2, 4, big, half), F32),
        vmem((1, 4, big, half), F32),
        vmem((1, 4, big, half), BF16),
        vmem((1, 4, half, half), BF16),
        vmem((2, 2, 1, half, half), BF16),
        vmem((2, 1, half, half), BF16),
        vmem((1, 2, half, half), BF16),
        vmem((2, 4, big, half), BF16),
        vmem((2, 4, half, half), BF16),
        vmem((2, 2, 2, half, half), BF16),
        vmem((2, 2, half, half), BF16),
        vmem((2, 2, half, half), BF16),
        pltpu.SemaphoreType.DMA((6,)),
        pltpu.SemaphoreType.DMA((COPIES,)),
        pltpu.SemaphoreType.DMA((COPIES,)),
    ]
    update = pl.pallas_call(
        functools.partial(kernel, n_row, n_col, slots, modes),
        out_shape=pltpu.VMEM((4 * extent, half), F32),
        in_specs=[anywhere] * 6,
        out_specs=pl.BlockSpec(memory_space=pltpu.VMEM),
        scratch_shapes=scratch,
        compiler_params=pltpu.CompilerParams(
            collective_id=0, has_side_effects=True, vmem_limit_bytes=56 * 1024 * 1024
        ),
        cost_estimate=pl.CostEstimate(flops=5 * 10**9, bytes_accessed=5 * 10**6, transcendentals=3 * 10**5),
    )(obj, probe, amplitudes[0], tab, positions.transpose(0, 2, 1), counts)
    return update.reshape(extent, 2, 2, half).transpose(0, 2, 1, 3).reshape(extent, 2, extent)


def solution(mesh):
    in_specs = (
        P("row", None, "col"),
        P(),
        P("row", "col", None, None),
        P("row", "col", None),
        P("row", "col"),
    )
    out_specs = P("row", None, "col")
    step = functools.partial(on_device, mesh.shape["row"], mesh.shape["col"])
    return jax.shard_map(step, mesh=mesh, in_specs=in_specs, out_specs=out_specs, check_vma=False)
```

```python
import functools

import jax
import jax.numpy as jnp
import numpy as np
from jax import lax
from jax.experimental import pallas as pl
from jax.experimental.pallas import tpu as pltpu
from jax.sharding import PartitionSpec as P

MESH = pl.DeviceIdType.MESH
F32 = jnp.float32
BF16 = jnp.bfloat16

floor_amplitude = 0.25
ridge_weight = 1.0

POS, CNT = 0, 1
OBJ = 2
CORNER = 8
AMP = 12
WEIGHT = 16
GRAD = 24
COPIES = 32
RIGHT, LEFT = (0, 1), (0, -1)


def tables(extent):
    half = extent // 2
    steps = np.arange(extent)
    turns = np.outer(np.arange(half), steps) % extent
    scale = 1.0 / np.sqrt(extent)
    cosine = np.cos(2.0 * np.pi * turns / extent) * scale
    sine = np.sin(2.0 * np.pi * turns / extent) * scale
    forward = []
    for parity in range(2):
        c, s = cosine[:, parity::2], sine[:, parity::2]
        forward.append(np.block([[c, -s], [s, c]]))
    order = np.concatenate([steps[0::2], steps[1::2]])
    permute = np.eye(extent)[order]
    stack = [forward[0], forward[1], forward[0].T, forward[1].T, permute, permute.T]
    return np.stack(stack).astype(np.float32).astype(jnp.bfloat16)


def dot(a, b):
    return jnp.dot(a, b, preferred_element_type=F32)


def kernel(
    n_row, n_col, slots, modes,
    obj_hbm, probe_hbm, amp_hbm, tab_hbm, pos_hbm, cnt_hbm, out,
    pos, cnt, obj, probe, amps, held, tab, pp, light, ext, win,
    rim, sa, ra, left_pos, left_cnt, table,
    far, ends, wave, near, stack, turned, grad, pg, pw, cv, cw,
    ws, wi, wx, wd, wo, gs, gi, gx, gd, go,
    lsem, ssem, rsem,
):
    row, col = lax.axis_index("row"), lax.axis_index("col")
    core = lax.rem(row, 2)
    outer, inner = 2 * core - 1, 1 - 2 * core
    has = {
        "right": col < n_col - 1, "left": col > 0,
        "outer": jnp.where(core == 0, row > 0, row < n_row - 1), "inner": row >= 0,
    }
    sides = (("right", 1), ("left", -1))

    def to(vertical, across):
        step = {"outer": outer, "inner": inner, "": 0}[vertical]
        return (row + step, col + {"right": 1, "left": -1, "": 0}[across])

    def exists(vertical, across):
        if vertical and across:
            return has[vertical] & has[across]
        return has[vertical or across]

    def opposite(across):
        return {"right": "left", "left": "right", "": ""}[across]

    def remote(number, src, dst, vertical, across):
        return pltpu.make_async_remote_copy(
            src_ref=src, dst_ref=dst, send_sem=ssem.at[number], recv_sem=rsem.at[number],
            device_id=to(vertical, across), device_id_type=MESH,
        )

    sent = {}

    def send(number, src, dst, vertical, across):
        copy = remote(number, src, dst, vertical, across)
        pl.when(exists(vertical, across))(copy.start)
        sent[number] = (copy, vertical, across)

    def arrived(number):
        copy, vertical, across = sent[number]
        pl.when(exists(vertical, opposite(across)))(copy.wait_recv)

    def rows(start):
        return pl.ds(pl.multiple_of(start, 128), 128)

    outer_half, inner_half = rows(128 + 128 * core), rows(256 - 128 * core)
    outer_rim, inner_rim = rows(384 * core), rows(384 - 384 * core)

    local = [
        pltpu.make_async_copy(obj_hbm, obj, lsem.at[0]),
        pltpu.make_async_copy(amp_hbm, amps, lsem.at[1]),
        pltpu.make_async_copy(probe_hbm, probe, lsem.at[2]),
        pltpu.make_async_copy(tab_hbm, tab, lsem.at[3]),
        pltpu.make_async_copy(pos_hbm, pos, lsem.at[4]),
        pltpu.make_async_copy(cnt_hbm, cnt, lsem.at[5]),
    ]
    for n in (0, 4, 5):
        local[n].start()

    barrier = pltpu.get_barrier_semaphore()
    for vertical, across in (("", "right"), ("", "left"), ("outer", ""), ("inner", "")):
        pl.when(exists(vertical, across))(
            functools.partial(
                pl.semaphore_signal, barrier, inc=1, device_id=to(vertical, across), device_id_type=MESH
            )
        )

    for c in range(2):
        for b in (0, 3):
            ext[c, b] = jnp.zeros((512, 128), F32)
        for b in (1, 2):
            ext[c, b, 0:128, :] = jnp.zeros((128, 128), F32)
            ext[c, b, 384:512, :] = jnp.zeros((128, 128), F32)
    local[0].wait()
    for n in (1, 3, 2):
        local[n].start()
    for c in range(2):
        for b in range(2):
            plane = obj[pl.ds(2 * b + c, 256, stride=4), :]
            ext[c, 1 + b, 128:384, :] = plane
            rim[c, 1 + b, 128:384, :] = plane.astype(BF16)

    neighbours = jnp.int32(1)
    for name in ("right", "left", "outer"):
        neighbours = neighbours + jnp.where(has[name], 1, 0)
    pl.semaphore_wait(barrier, neighbours)

    local[4].wait()
    local[5].wait()
    send(POS, pos, left_pos, "", "right")
    send(CNT, cnt, left_cnt, "", "right")
    for n, half in enumerate((outer_half, inner_half)):
        send(OBJ + 2 * n, rim.at[:, 2, half], rim.at[:, 0, half], "", "right")
        send(OBJ + 2 * n + 1, rim.at[:, 1, half], rim.at[:, 3, half], "", "left")
    send(OBJ + 4, rim.at[:, pl.ds(1, 2), outer_half], rim.at[:, pl.ds(1, 2), inner_rim], "outer", "")
    send(OBJ + 5, rim.at[:, pl.ds(1, 2), inner_half], rim.at[:, pl.ds(1, 2), outer_rim], "inner", "")

    def widen(number, blocks, span):
        copy, vertical, across = sent[number]

        @pl.when(exists(vertical, opposite(across)))
        def _():
            copy.wait_recv()
            for c in range(2):
                for b in blocks:
                    ext[c, b, span, :] = rim[c, b, span, :].astype(F32)

    def corners(n, half, beyond, vertical):
        for m, (side, block) in enumerate((("left", 0), ("right", 3))):
            widen(OBJ + 2 * n + m, [block], half)
            copy = remote(CORNER + 2 * n + m, rim.at[:, block, half], rim.at[:, block, beyond], vertical, "")
            there = exists(vertical, side)
            pl.when(there)(copy.start)
            corner_copies.append((copy, there, block, vertical))

    corner_copies = []

    def ranked(ref, count, tile):
        rank = jnp.int32(0)
        picked = [[jnp.int32(0)] * 3 for _ in range(4)]
        for i in range(slots):
            y, x = ref[0, 0, i], ref[0, 1, i]
            here = jnp.where((i < count) & ((x >> 8) == tile), 1, 0)
            for j in range(4):
                hit = jnp.where(rank == j, here, 0)
                picked[j] = [old + hit * new for old, new in zip(picked[j], (i, y, x))]
            rank = rank + here
        return picked, rank

    def reorder(picked, there):
        halves = [dot(tab[4], amps[picked[j][0] & (slots - 1)]).astype(BF16) for j in range(4)]
        for j in range(4):
            there[j] = dot(halves[j], tab[5]).astype(BF16)

    going, _ = ranked(pos, cnt[0, 0], col + 1)
    local[1].wait()
    local[3].wait()
    reorder(going, sa)
    for j in range(1):
        send(AMP + j, sa.at[j], ra.at[j], "", "right")
    home, n_home = ranked(pos, cnt[0, 0], col)
    reorder(home, held)
    corners(0, outer_half, inner_rim, "outer")

    local[2].wait()
    for k in range(modes):
        for c in range(2):
            for b in range(2):
                pp[k, c, b] = probe[pl.ds(k * 1024 + 2 * b + c, 256, stride=4), :]
    for b in range(2):
        for first in range(0, 256, 32):
            total = None
            for k in range(modes):
                for c in range(2):
                    part = pp[k, c, b, first : first + 32, :]
                    total = part * part if total is None else total + part * part
            light[b, first : first + 32, :] = total

    for c in range(2):
        pg[c, 12] = jnp.zeros((768, 128), F32)
        for n in range(12):
            for first in (0, 512):
                pg[c, n, first : first + 256, :] = jnp.zeros((256, 128), F32)
    pw[...] = jnp.zeros_like(pw)
    cw[...] = jnp.zeros_like(cw)
    for j in range(4):
        held[4 + j] = jnp.zeros((256, 256), BF16)

    for side in range(2):

        @pl.when(jnp.logical_not(has[("left", "right")[side]]))
        def _(side=side):
            for ref in (wx, gx):
                ref[:, side] = jnp.zeros(ref.shape[:1] + ref.shape[2:], BF16)

        @pl.when(jnp.logical_not(exists("outer", ("left", "right")[side])))
        def _(side=side):
            for ref in (wd, gd):
                ref[side] = jnp.zeros(ref.shape[1:], BF16)

    @pl.when(jnp.logical_not(has["outer"]))
    def _():
        for ref in (wo, go):
            ref[...] = jnp.zeros(ref.shape, BF16)

    corners(1, inner_half, outer_rim, "inner")
    for j in range(1, 4):
        send(AMP + j, sa.at[j], ra.at[j], "", "right")

    arrived(POS)
    arrived(CNT)

    @pl.when(jnp.logical_not(has["left"]))
    def _():
        left_cnt[0, 0] = 0
        for i in range(slots):
            for axis in range(2):
                left_pos[0, axis, i] = 0

    came, _ = ranked(left_pos, left_cnt[0, 0], col)
    for j in range(4):
        for i in range(2):
            table[3 + i, j] = came[j][1 + i]
    for j in range(4):
        from_left = j >= n_home
        there = jnp.clip(j - n_home, 0, 3)
        table[0, j] = jnp.where(from_left, 4 + there, j)
        for i in range(2):
            table[1 + i, j] = jnp.where(from_left, table[3 + i, there], home[j][1 + i]) & 255

    lanes = lax.broadcasted_iota(jnp.int32, (256, 128), 1)

    def spread(ref, pieces, shift):
        keep = lanes >= shift
        low, high = (pltpu.roll(piece, shift, 1) for piece in pieces)
        ref[1, 256:512, :] = jnp.where(keep, low, 0.0)
        ref[2, 256:512, :] = jnp.where(keep, high, low)
        ref[3, 256:512, :] = jnp.where(keep, 0.0, high)

    def place(canvas, ref, y, block):
        for b in range(4):
            canvas[b] += ref[b - block + 1, pl.ds(256 - y, 512), :]

    def weigh(j, carry):
        y, x = table[1, j], table[2, j]
        spread(pw, [light[0], light[1]], x & 127)
        place(cw.at[0], pw, y, x >> 7)
        return carry

    lax.fori_loop(0, 4, weigh, 0)
    for b in range(4):
        ws[0, b] = cw[0, b].astype(BF16)

    widen(OBJ + 4, [1, 2], outer_rim)
    widen(OBJ + 5, [1, 2], inner_rim)
    for copy, there, block, vertical in corner_copies:
        span = outer_rim if vertical == "outer" else inner_rim

        @pl.when(there)
        def _(copy=copy, block=block, span=span):
            copy.wait_recv()
            for c in range(2):
                ext[c, block, span, :] = rim[c, block, span, :].astype(F32)

    def halo_out(base, gather, layers, stage, from_inner, from_x, from_corner, from_outer, ready=False):
        def rounded(blocks, span):
            for c in range(0 if ready else layers):
                for b in blocks:
                    stage[c, b, span, :] = gather(c, b, span).astype(BF16)

        rounded(range(4), inner_rim)
        send(base, stage.at[:, :, inner_rim], from_inner, "inner", "")
        rounded((0, 3), outer_half)
        for n, (side, block) in enumerate((("right", 3), ("left", 0))):
            send(base + 1 + n, stage.at[:, block, outer_half], from_x.at[0, n], "", side)
        rounded(range(4), outer_rim)
        for n, (side, block) in enumerate((("right", 3), ("left", 0))):
            send(base + 3 + n, stage.at[:, block, outer_rim], from_corner.at[n], "outer", side)
        send(base + 5, stage.at[:, pl.ds(1, 2), outer_rim], from_outer, "outer", "")

    def halo_inner(base, gather, layers, stage, from_inner, from_x):
        arrived(base)
        for n, (side, block) in enumerate((("right", 3), ("left", 0))):
            for c in range(layers):
                total = gather(c, block, inner_half) + from_inner[c, block].astype(F32)
                stage[c, block, inner_half, :] = total.astype(BF16)
            send(base + 6 + n, stage.at[:, block, inner_half], from_x.at[1, n], "", side)

    def weight_at(c, b, span):
        return cw[c, b, span, :]

    halo_out(WEIGHT, weight_at, 1, ws, wi, wx, wd, wo, True)

    def cut_window(j):
        y, x = table[1, j], table[2, j]
        block, shift = x >> 7, x & 127
        keep = lax.broadcasted_iota(jnp.int32, (64, 128), 1) >= shift
        for c in range(2):
            for b in range(2):
                for first in range(0, 256, 64):
                    near = ext[c, block + b, pl.ds(y + first, 64), :]
                    beyond = ext[c, block + b + 1, pl.ds(y + first, 64), :]
                    win[c, b, first : first + 64, :] = pltpu.roll(
                        jnp.where(keep, near, beyond), (128 - shift) & 127, 1
                    )


    def exit_waves():
        def piece(first):
            cut = slice(first, first + 16)
            at = 2 * first if first < 128 else 2 * (first - 128) + 16
            w_re, w_im = [win[0, b, cut, :] for b in range(2)], [win[1, b, cut, :] for b in range(2)]
            for k in range(modes):
                waves = []
                for b in range(2):
                    p_re, p_im = pp[k, 0, b, cut, :], pp[k, 1, b, cut, :]
                    waves.append((p_re * w_re[b] - p_im * w_im[b], p_re * w_im[b] + p_im * w_re[b]))
                to_rows = slice(256 * k + at, 256 * k + at + 16)
                for part in range(2):
                    low, high = waves[0][part], waves[1][part]
                    lanes_of = slice(128 * part, 128 * part + 128)
                    wave[0, to_rows, lanes_of] = (low + high).astype(BF16)
                    wave[1, to_rows, lanes_of] = (low - high).astype(BF16)

        return [functools.partial(piece, first) for first in range(0, 256, 16)]

    def half_done():
        done = {}

        def product(parity):
            done[parity] = dot(wave[parity], tab[parity])

        def piece(parity, k, first):
            lanes_of = slice(128 * parity, 128 * parity + 128)
            at = 256 * k + 2 * first
            low, high = done[parity][at : at + 16], done[parity][at + 16 : at + 32]
            plus, minus = (low + high).astype(BF16), (low - high).astype(BF16)
            for part in range(2):
                to_rows = slice(128 * part + first, 128 * part + first + 16)
                source = slice(128 * part, 128 * part + 128)
                stack[0, k, to_rows, lanes_of] = plus[:, source]
                stack[1, k, to_rows, lanes_of] = minus[:, source]

        pieces = []
        for parity in range(2):
            pieces.append(functools.partial(product, parity))
            pieces += [functools.partial(piece, parity, k, f) for k in range(modes) for f in range(0, 128, 16)]
        return pieces

    def far_field():
        def piece(parity, k):
            far[parity, k] = dot(tab[2 + parity], stack[parity, k])

        return [functools.partial(piece, parity, k) for parity in range(2) for k in range(modes)]

    def residue(parity, amplitude):
        for first in range(0, 128, 16):
            upper, lower = slice(first, first + 16), slice(128 + first, 144 + first)
            re = [far[parity, k, upper, :] for k in range(modes)]
            im = [far[parity, k, lower, :] for k in range(modes)]
            intensity = None
            for k in range(modes):
                term = re[k] * re[k] + im[k] * im[k]
                intensity = term if intensity is None else intensity + term
            held = lax.rsqrt(jnp.maximum(intensity, floor_amplitude * floor_amplitude))
            measured = amplitude[128 * parity + first : 128 * parity + first + 16, :].astype(F32)
            factor = 1.0 - measured * held
            for k in range(modes):
                turned[parity, k, upper, :] = (re[k] * factor).astype(BF16)
                turned[parity, k, lower, :] = (im[k] * factor).astype(BF16)

    def near_field():
        done = {}

        def product(parity, k):
            done[parity, k] = dot(tab[parity], turned[parity, k])

        def piece(k, first):
            cut = slice(first, first + 16)
            part, at = first // 128, 256 * k + first % 128
            lanes_of = slice(128 * part, 128 * part + 128)
            even, odd = done[0, k][cut], done[1, k][cut]
            plus, minus = (even + odd).astype(BF16), (even - odd).astype(BF16)
            for column in range(2):
                source = slice(128 * column, 128 * column + 128)
                near[column, at : at + 16, lanes_of] = plus[:, source]
                near[column, 128 + at : 144 + at, lanes_of] = minus[:, source]

        pieces = []
        for k in range(modes):
            pieces += [functools.partial(product, parity, k) for parity in range(2)]
            pieces += [functools.partial(piece, k, first) for first in range(0, 256, 16)]
        return pieces

    def back_parts():
        def piece(parity):
            back = dot(near[parity], tab[2 + parity])
            for k in range(modes):
                ends[parity, k] = back[256 * k : 256 * k + 256]

        return [functools.partial(piece, parity) for parity in range(2)]

    def gradient():
        def piece(first):
            cut = slice(first, first + 16)
            total = [None] * 4
            for k in range(modes):
                e_re, o_re = ends[0, k, cut, 0:128], ends[1, k, cut, 0:128]
                e_im, o_im = ends[0, k, cut, 128:256], ends[1, k, cut, 128:256]
                for b in range(2):
                    b_re = e_re + o_re if b == 0 else e_re - o_re
                    b_im = e_im + o_im if b == 0 else e_im - o_im
                    p_re, p_im = pp[k, 0, b, cut, :], pp[k, 1, b, cut, :]
                    for n, term in ((b, p_re * b_re + p_im * b_im), (2 + b, p_re * b_im - p_im * b_re)):
                        total[n] = term if total[n] is None else total[n] + term
            for b in range(2):
                grad[0, b, cut, :] = total[b]
                grad[1, b, cut, :] = total[2 + b]

        return [functools.partial(piece, first) for first in range(0, 256, 16)]

    def take_turns(*stages):
        marked = [((n + 0.5) / len(stage), m, piece) for m, stage in enumerate(stages) for n, piece in enumerate(stage)]
        for _, _, piece in sorted(marked, key=lambda entry: entry[:2]):
            piece()

    def keep_gradient(j):
        shift = table[2, j] & 127
        for first in range(0, 256, 64):
            cut, at = slice(first, first + 64), slice(256 + first, 320 + first)
            keep = lax.broadcasted_iota(jnp.int32, (64, 128), 1) >= shift
            for c in range(2):
                low, high = (pltpu.roll(grad[c, b, cut, :], shift, 1) for b in range(2))
                pg[c, 3 * j, at, :] = jnp.where(keep, low, 0.0)
                pg[c, 3 * j + 1, at, :] = jnp.where(keep, high, low)
                pg[c, 3 * j + 2, at, :] = jnp.where(keep, 0.0, high)

    def start_window(j):
        cut_window(j)
        take_turns(exit_waves())
        take_turns(half_done())
        take_turns(far_field())

    def factor_window(j):
        @pl.when(has["left"])
        def _():
            remote(AMP + j, sa.at[j], ra.at[j], "", "right").wait_recv()
            held[4 + j] = ra[j]

        amplitude = held.at[table[0, j]]
        for parity in range(2):
            residue(parity, amplitude)

    def slot(j, carry):
        factor_window(j)
        cut_window(j + 1)
        take_turns(near_field(), exit_waves())
        take_turns(half_done())
        take_turns(back_parts())
        take_turns(far_field(), gradient())
        keep_gradient(j)
        return carry

    start_window(0)
    lax.fori_loop(0, 3, slot, 0)
    halo_inner(WEIGHT, weight_at, 1, ws, wi, wx)
    factor_window(3)
    for stage in (near_field, back_parts, gradient):
        take_turns(stage())
    keep_gradient(3)

    def gradient_at(c, b, span):
        total = None
        for j in range(4):
            y, block = table[1, j], table[2, j] >> 7
            inside = (b >= block) & (b < block + 3)
            part = pg[c, jnp.where(inside, 3 * j + b - block, 12), pl.ds(256 - y + span.start, 128), :]
            total = part if total is None else total + part
        return total

    halo_out(GRAD, gradient_at, 2, gs, gi, gx, gd, go)
    halo_inner(GRAD, gradient_at, 2, gs, gi, gx)

    def whole(gather, c, b, from_inner, from_x, from_corner, from_outer):
        total = gather(c, 1 + b, outer_half) + from_outer[c, b].astype(F32)
        total = total + from_x[0, b, c].astype(F32) + from_corner[b, c].astype(F32)
        other = gather(c, 1 + b, inner_half) + from_inner[c, 1 + b].astype(F32)
        return total, other + from_x[1, b, c].astype(F32)

    for c in range(2):
        for b in (1, 2):
            for span in (outer_half, inner_half):
                cv[c, b, span, :] = gradient_at(c, b, span)

    def own_gradient(c, b, span):
        return cv[c, b, span, :]

    for number in range(1, 8):
        arrived(WEIGHT + number)
    for b in range(2):
        far_half, near_half = whole(weight_at, 0, b, wi, wx, wd, wo)
        cw[0, 1 + b, outer_half, :] = 1.0 / (far_half + ridge_weight)
        cw[0, 1 + b, inner_half, :] = 1.0 / (near_half + ridge_weight)
    for number in range(1, 8):
        arrived(GRAD + number)
    for c in range(2):
        for b in range(2):
            far_half, near_half = whole(own_gradient, c, b, gi, gx, gd, go)
            first, second = 512 * core + 2 * b + c, 512 - 512 * core + 2 * b + c
            out[pl.ds(first, 128, stride=4), :] = far_half * cw[0, 1 + b, outer_half, :]
            out[pl.ds(second, 128, stride=4), :] = near_half * cw[0, 1 + b, inner_half, :]

    for copy, vertical, across in sent.values():
        pl.when(exists(vertical, across))(copy.wait_send)
    for copy, there, _, _ in corner_copies:
        pl.when(there)(copy.wait_send)


def on_device(n_row, n_col, object_field, probe_modes, amplitudes, positions, counts):
    modes, extent = probe_modes.shape[0], probe_modes.shape[1]
    slots = amplitudes.shape[1]
    half = extent // 2
    obj = object_field.reshape(extent, 2, 2, half).transpose(0, 2, 1, 3).reshape(4 * extent, half)
    probe = probe_modes.reshape(modes, extent, 2, 2, half).transpose(0, 1, 3, 2, 4)
    probe = probe.reshape(modes * 4 * extent, half)
    tab = jnp.asarray(tables(extent))
    big = 2 * extent
    vmem, anywhere = pltpu.VMEM, pl.BlockSpec(memory_space=pl.ANY)
    scratch = [
        pltpu.SMEM((1, 2, slots), jnp.int32),
        pltpu.SMEM((1, 1), jnp.int32),
        vmem((4 * extent, half), F32),
        vmem((modes * 4 * extent, half), F32),
        vmem((slots, extent, extent), BF16),
        vmem((8, extent, extent), BF16),
        vmem((6, extent, extent), BF16),
        vmem((modes, 2, 2, extent, half), F32),
        vmem((2, extent, half), F32),
        vmem((2, 4, big, half), F32),
        vmem((2, 2, extent, half), F32),
        vmem((2, 4, big, half), BF16),
        vmem((4, extent, extent), BF16),
        vmem((4, extent, extent), BF16),
        pltpu.SMEM((1, 2, slots), jnp.int32),
        pltpu.SMEM((1, 1), jnp.int32),
        pltpu.SMEM((5, 4), jnp.int32),
        vmem((2, modes, extent, extent), F32),
        vmem((2, modes, extent, extent), F32),
        vmem((2, modes * extent, extent), BF16),
        vmem((2, modes * extent, extent), BF16),
        vmem((2, modes, extent, extent), BF16),
        vmem((2, modes, extent, extent), BF16),
        vmem((2, 2, extent, half), F32),
        vmem((2, 13, 3 * extent, half), F32),
        vmem((5, 3 * extent, half), F32),
        vmem((2, 4, big, half), F32),
        vmem((1, 4, big, half), F32),
        vmem((1, 4, big, half), BF16),
        vmem((1, 4, half, half), BF16),
        vmem((2, 2, 1, half, half), BF16),
        vmem((2, 1, half, half), BF16),
        vmem((1, 2, half, half), BF16),
        vmem((2, 4, big, half), BF16),
        vmem((2, 4, half, half), BF16),
        vmem((2, 2, 2, half, half), BF16),
        vmem((2, 2, half, half), BF16),
        vmem((2, 2, half, half), BF16),
        pltpu.SemaphoreType.DMA((6,)),
        pltpu.SemaphoreType.DMA((COPIES,)),
        pltpu.SemaphoreType.DMA((COPIES,)),
    ]
    update = pl.pallas_call(
        functools.partial(kernel, n_row, n_col, slots, modes),
        out_shape=pltpu.VMEM((4 * extent, half), F32),
        in_specs=[anywhere] * 6,
        out_specs=pl.BlockSpec(memory_space=pltpu.VMEM),
        scratch_shapes=scratch,
        compiler_params=pltpu.CompilerParams(
            collective_id=0, has_side_effects=True, vmem_limit_bytes=56 * 1024 * 1024
        ),
        cost_estimate=pl.CostEstimate(flops=5 * 10**9, bytes_accessed=5 * 10**6, transcendentals=3 * 10**5),
    )(obj, probe, amplitudes[0], tab, positions.transpose(0, 2, 1), counts)
    return update.reshape(extent, 2, 2, half).transpose(0, 2, 1, 3).reshape(extent, 2, extent)


def solution(mesh):
    in_specs = (
        P("row", None, "col"),
        P(),
        P("row", "col", None, None),
        P("row", "col", None),
        P("row", "col"),
    )
    out_specs = P("row", None, "col")
    step = functools.partial(on_device, mesh.shape["row"], mesh.shape["col"])
    return jax.shard_map(step, mesh=mesh, in_specs=in_specs, out_specs=out_specs, check_vma=False)
```
